256 devices in a mesh: dp: 16 (over z_hi, x), fsdp: 16 (over y, z_lo, core).
Axes of the slice: x: 4, y: 4, z: 8 (z_hi: 4, z_lo: 2; z = z_hi * 2 + z_lo), core: 2. Of those that a mesh axis runs over, the one named last changes fastest.
Arguments:
- hidden: bfloat16 [12288, 14336], P('fsdp', 'dp'), may hold values from -6 to 6
- cotangent: bfloat16 [12288, 4096], P('fsdp'), may hold values from -6 to 6
- weight: bfloat16 [14336, 4096], P('dp', 'fsdp'), may hold values from -0.0625 to 0.0625
- basis: bfloat16 [14336, 512], P('dp'), may hold values from -0.0625 to 0.0625
- first_moment: float32 [512, 4096], P('dp', 'fsdp'), may hold values from -665.1075 to 665.1075
- second_moment: float32 [512, 4096], P('dp', 'fsdp'), may hold values from 13 to 3076
Outputs:
- output: bfloat16 [12288, 4096], P('fsdp', 'dp')
- act_grad: bfloat16 [12288, 14336], P('fsdp', 'dp')
- new_first: float32 [512, 4096], P('dp', 'fsdp')
- new_second: float32 [512, 4096], P('dp', 'fsdp')
- update: bfloat16 [14336, 4096], P('dp', 'fsdp')
The draws below stay inside these ranges and needn't reach their ends.
All inputs are finite; a program needn't handle non-finite values.
Results may differ from the reference program's by a relative error of at most 0.0051.
Values may be sent and summed in bfloat16 or wider, within the bound.
No kernel may reach another device: no remote copies, remote signals or barrier semaphores. Data moves between devices by JAX's collectives and lax.ppermute only.
A program may use at most 128 MiB of HBM per device.

```python
import math
import jax
import jax.numpy as jnp
from jax import lax

D = 4096
FF = 14336
RANK = 512
STEP = 20
TOKENS = 12288


def spiked(result, key, source, target, shards_of, factor):
    owner, partner = [(jnp.arange(result.shape[dim]) // (result.shape[dim] // shards_of)).reshape([-1 if axis == dim else 1 for axis in range(result.ndim)]) for dim in (source, target)]
    chosen = jax.random.permutation(key, shards_of)[partner]
    strong = (owner == chosen) | (owner == (partner + shards_of // 2) % shards_of)
    return jnp.where(strong, factor * result, result)


def level_of(stream_key, extent, pieces, low, top_value):
    gain = 1.0
    for dim, blocks in pieces:
        draws = jax.random.uniform(jax.random.fold_in(jax.random.fold_in(stream_key, 6), dim), (blocks,), jnp.float32, low / len(pieces), top_value / len(pieces))
        gain = gain * jnp.repeat(jnp.exp(draws), extent[dim] // blocks).reshape((-1,) + (1,) * (len(extent) - 1 - dim))
    return gain


def bell_draw(rng, shape, scale, limit, split=(), kind=jnp.bfloat16):
    entries = jax.random.normal(rng, shape, jnp.float32) * scale
    if len(split) > 0:
        entries = level_of(rng, shape, split, -0.22, 0.18) * entries
    return jnp.clip(entries, min=-limit, max=limit).astype(kind)


def bell_draw_with(key, shape, deviation, bound, shards, heavy, held_as=jnp.bfloat16):
    result = deviation * jax.random.normal(key, shape, jnp.float32)
    if shards:
        result = result * level_of(key, shape, shards, -0.22, 0.18)
    return jnp.clip(spiked(result, jax.random.fold_in(key, 3), *heavy), -bound, bound).astype(held_as)


def setup_inputs(seed: int = 0) -> dict:
    seeds = jax.random.split(jax.random.key(seed), 7)
    hidden = bell_draw(seeds[0], (TOKENS, FF), 1.0, 6.0, ((0, 16), (1, 16)))
    cotangent = bell_draw_with(seeds[1], (TOKENS, D), 1.0, 6.0, ((0, 16),), (0, 1, 16, 2.0))
    weight = bell_draw_with(seeds[2], (FF, D), FF ** -0.5, 0.0625, ((0, 16), (1, 16)), (0, 1, 16, 2.0))
    basis = bell_draw_with(seeds[3], (FF, RANK), FF ** -0.5, 0.0625, ((0, 16),), (0, 1, 16, 2.0))
    first_moment = bell_draw(seeds[4], (RANK, D), (TOKENS ** 0.5), 665.1075, ((0, 16), (1, 16)), jnp.float32)
    second_moment = jnp.clip(jnp.exp(math.log(3076.0) - 5.466436 * jax.random.uniform(seeds[5], (RANK, D), jnp.float32) ** level_of(seeds[5], (RANK, D), ((0, 16), (1, 16)), -0.2, 0.2)), 13.0, 3076.0)
    return dict(hidden=hidden, cotangent=cotangent, weight=weight, basis=basis, first_moment=first_moment, second_moment=second_moment)


def reference(hidden, cotangent, weight, basis, first_moment, second_moment):
    output = jnp.dot(hidden, weight, preferred_element_type=jnp.float32).astype(jnp.bfloat16)
    act_grad = lax.dot_general(cotangent, weight, (((1,), (1,)), ((), ())), preferred_element_type=jnp.float32).astype(jnp.bfloat16)
    low = jnp.dot(hidden, basis, preferred_element_type=jnp.float32).astype(jnp.bfloat16)
    grad = lax.dot_general(low, cotangent, (((0,), (0,)), ((), ())), preferred_element_type=jnp.float32)
    new_first = 0.9 * first_moment + 0.1 * grad
    new_second = 0.999 * second_moment + 0.001 * grad * grad
    first_fix = 1.0 - 0.9 ** STEP
    second_fix = 1.0 - 0.999 ** STEP
    normed = (new_first / first_fix / (jnp.sqrt(new_second / second_fix) + 1e-08)).astype(jnp.bfloat16)
    update = jnp.dot(basis, normed, preferred_element_type=jnp.float32).astype(jnp.bfloat16)
    return (output, act_grad, new_first, new_second, update)
```

```python
import functools

import jax
import jax.numpy as jnp
from jax import lax
from jax.experimental import pallas as pl
from jax.experimental.pallas import tpu as pltpu
from jax.sharding import Mesh
from jax.sharding import PartitionSpec as P

STEP = 20
BF = jnp.bfloat16
F32 = jnp.float32
AXES = ("zh", "x", "y", "zl", "c")
SIZE = dict(zh=4, x=4, y=4, zl=2, c=2)
GROUPS = (
    (0, 512, ((0,), (1, 3), (2,))),
    (512, 256, ((0, 1, 3, 2),)),
)
VMEM_LIMIT = 48 * 1024 * 1024
FULL = pl.BlockSpec(memory_space=pltpu.VMEM)
SCALARS = pl.BlockSpec(memory_space=pltpu.SMEM)


def shift(array, axis, by):
    n = SIZE[axis]
    return lax.ppermute(array, axis, [(i, (i + by) % n) for i in range(n)])


def params():
    return pltpu.CompilerParams(vmem_limit_bytes=VMEM_LIMIT)


def partial_kernel(m, half, pick, h_ref, *refs):
    w_refs = refs[: 4 * m]
    far_up, far_down, near_up, near_down, acc_up, acc_down, own, chosen = refs[4 * m :]
    wide = m * 256
    for k in range(4):
        for block in range(m):
            for slot in range(4):

                @pl.when(pick[k] == slot)
                def _(k=k, block=block, slot=slot):
                    start = k * wide + block * 256
                    chosen[:, start : start + 256] = w_refs[4 * block + slot][...]

    def product(k):
        return jnp.dot(
            h_ref[...], chosen[:, k * wide : (k + 1) * wide], preferred_element_type=F32
        )

    res = product(0)
    far_up[...] = res[:half].astype(BF)
    far_down[...] = res[half:].astype(BF)
    res = product(1)
    acc_up[...] = res[:half]
    near_up[...] = res[half:].astype(BF)
    res = product(2)
    near_down[...] = res[:half].astype(BF)
    acc_down[...] = res[half:]
    own[...] = product(3)


def partials(hidden, shards, pick, start, rows):
    m = len(shards)
    half = rows // 2
    wide = m * 256
    flat = [w for four in shards for w in four]
    small = jax.ShapeDtypeStruct((half, wide), BF)
    kept = jax.ShapeDtypeStruct((half, wide), F32)
    whole = jax.ShapeDtypeStruct((rows, wide), F32)
    full = hidden.shape[1]

    def same(i, s):
        return (0, 0)

    return pl.pallas_call(
        functools.partial(partial_kernel, m, half),
        out_shape=[small] * 4 + [kept] * 2 + [whole],
        grid_spec=pltpu.PrefetchScalarGridSpec(
            num_scalar_prefetch=1,
            grid=(1,),
            in_specs=[pl.BlockSpec((rows, full), lambda i, s: (start // rows, 0))]
            + [pl.BlockSpec((full, 256), same)] * len(flat),
            out_specs=[pl.BlockSpec((half, wide), same)] * 6 + [pl.BlockSpec((rows, wide), same)],
            scratch_shapes=[pltpu.VMEM((full, 4 * wide), BF)],
        ),
        compiler_params=params(),
        cost_estimate=pl.CostEstimate(
            flops=2 * rows * full * 4 * wide, bytes_accessed=full * wide * 8 + rows * wide * 16, transcendentals=0
        ),
        name="partials",
    )(pick, hidden, *flat)


def add_kernel(a, b, ra, rb, out_a, out_b):
    out_a[...] = (a[...] + ra[...].astype(F32)).astype(BF)
    out_b[...] = (b[...] + rb[...].astype(F32)).astype(BF)


def add_pair(a, b, ra, rb):
    return pl.pallas_call(
        add_kernel,
        out_shape=[jax.ShapeDtypeStruct(a.shape, BF)] * 2,
        in_specs=[FULL] * 4,
        out_specs=[FULL] * 2,
        compiler_params=params(),
        cost_estimate=pl.CostEstimate(flops=2 * a.size, bytes_accessed=16 * a.size, transcendentals=0),
        name="add_pair",
    )(a, b, ra, rb)


def ring(axis, far_up, far_down, near_up, near_down, acc_up, acc_down):
    got_far_up = shift(far_up, axis, 1)
    got_far_down = shift(far_down, axis, -1)
    got_near_up = shift(near_up, axis, 1)
    got_near_down = shift(near_down, axis, -1)
    last_up, last_down = add_pair(acc_up, acc_down, got_far_up, got_far_down)
    got_last_up = shift(last_up, axis, 1)
    got_last_down = shift(last_down, axis, -1)
    return got_last_up, got_near_down, got_near_up, got_last_down


def regroup_kernel(sets, half, pick, *refs):
    parts = refs[: 5 * len(sets)]
    far_up, far_down, near_up, near_down, acc_up, acc_down, own = refs[5 * len(sets) :]
    for k in range(4):
        for s, offsets in enumerate(sets):
            mine, last_up, near_dn, near_u, last_dn = parts[5 * s : 5 * s + 5]
            for block, offset in enumerate(offsets):

                @pl.when(pick[k] == offset)
                def _(k=k, block=block, mine=mine, last_up=last_up, near_dn=near_dn, near_u=near_u, last_dn=last_dn):
                    cols = slice(block * 256, block * 256 + 256)
                    top = mine[:half, cols] + last_up[:, cols].astype(F32) + near_dn[:, cols].astype(F32)
                    low = mine[half:, cols] + near_u[:, cols].astype(F32) + last_dn[:, cols].astype(F32)
                    if k == 0:
                        far_up[...] = top.astype(BF)
                        far_down[...] = low.astype(BF)
                    elif k == 1:
                        acc_up[...] = top
                        near_up[...] = low.astype(BF)
                    elif k == 2:
                        near_down[...] = top.astype(BF)
                        acc_down[...] = low
                    else:
                        own[:half] = top
                        own[half:] = low


def regroup(parts, sets, pick, rows):
    half = rows // 2
    small = jax.ShapeDtypeStruct((half, 256), BF)
    kept = jax.ShapeDtypeStruct((half, 256), F32)
    whole = jax.ShapeDtypeStruct((rows, 256), F32)
    return pl.pallas_call(
        functools.partial(regroup_kernel, sets, half),
        out_shape=[small] * 4 + [kept] * 2 + [whole],
        in_specs=[SCALARS] + [FULL] * len(parts),
        out_specs=[FULL] * 7,
        compiler_params=params(),
        cost_estimate=pl.CostEstimate(flops=rows * 4096, bytes_accessed=rows * 8192, transcendentals=0),
        name="regroup",
    )(pick, *parts)


def act_kernel(order, cot_ref, *refs):
    w_refs, out_ref = refs[:16], refs[16]
    total = jnp.zeros(out_ref.shape, F32)
    for s in range(16):
        at = pl.multiple_of(order[s] * 256, 256)
        total += lax.dot_general(
            cot_ref[:, pl.ds(at, 256)],
            w_refs[s][...],
            (((1,), (1,)), ((), ())),
            preferred_element_type=F32,
        )
    out_ref[...] = total.astype(BF)


def act(cotangent, shards, order):
    tokens, features = cotangent.shape
    rows = 256
    full = shards[0].shape[0]
    return pl.pallas_call(
        act_kernel,
        out_shape=jax.ShapeDtypeStruct((tokens, full), BF),
        grid_spec=pltpu.PrefetchScalarGridSpec(
            num_scalar_prefetch=1,
            grid=(tokens // rows,),
            in_specs=[pl.BlockSpec((rows, features), lambda i, s: (i, 0))]
            + [pl.BlockSpec((full, 256), lambda i, s: (0, 0))] * 16,
            out_specs=pl.BlockSpec((rows, full), lambda i, s: (i, 0)),
        ),
        compiler_params=params(),
        cost_estimate=pl.CostEstimate(
            flops=2 * tokens * features * full, bytes_accessed=16 * 1024 * 1024, transcendentals=0
        ),
        name="act_grad",
    )(order, cotangent, *shards)


def gather_rows(block, axis, at):
    n = SIZE[axis]
    pieces = [block] + [shift(block, axis, -k) for k in range(1, n)]
    twice = jnp.concatenate(pieces + pieces, axis=0)
    rows = block.shape[0]
    return lax.dynamic_slice_in_dim(twice, ((n - at) % n) * rows, n * rows, 0)


def on_device(hidden, cotangent, weight, basis, first_moment, second_moment):
    zh, x, y, zl, c = (lax.axis_index(a) for a in AXES)

    side = shift(weight, "zl", 1)
    next0 = shift(weight, "y", -1)
    prev0 = shift(weight, "y", 1)
    next1 = shift(side, "y", -1)
    prev1 = shift(side, "y", 1)
    far0 = shift(next0, "y", -1)
    far1 = shift(prev1, "y", 1)
    held = {0: (weight, side), 1: (next0, next1), 3: (prev0, prev1), 2: (far0, far1)}
    slots = {
        off: (own, shift(own, "c", 1), other, shift(other, "c", 1)) for off, (own, other) in held.items()
    }

    low_part = lax.dot_general(
        basis, hidden, (((0,), (1,)), ((), ())), preferred_element_type=F32
    ).astype(BF)
    tokens = hidden.shape[0]
    low4 = low_part.reshape(4, 4, 32, tokens)

    def low_to(k):
        return lax.dynamic_index_in_dim(low4, (x + k) % 4, 1, keepdims=False)

    low_x = low_to(0).astype(F32)
    for k in (1, 2, 3):
        low_x = low_x + shift(low_to(k), "x", k).astype(F32)
    low_xb = low_x.astype(BF)

    def low_zto(k):
        return lax.dynamic_index_in_dim(low_xb, (zh + k) % 4, 0, keepdims=False)

    low = lax.dynamic_index_in_dim(low_x, zh, 0, keepdims=False)
    for k in (1, 2, 3):
        low = low + shift(low_zto(k), "zh", k).astype(F32)
    low = low.astype(BF)

    grad_part = jnp.dot(low, cotangent, preferred_element_type=F32)
    g = grad_part.reshape(32, 8, 2, 256)
    g = lax.dynamic_index_in_dim(g, c, 2, keepdims=False) + shift(
        lax.dynamic_index_in_dim(g, 1 - c, 2, keepdims=False), "c", 1
    )
    g = g.reshape(32, 4, 2, 256)
    g = lax.dynamic_index_in_dim(g, zl, 2, keepdims=False) + shift(
        lax.dynamic_index_in_dim(g, 1 - zl, 2, keepdims=False), "zl", 1
    )
    grad = lax.dynamic_index_in_dim(g, y, 1, keepdims=False)
    for k in (1, 2, 3):
        grad = grad + shift(lax.dynamic_index_in_dim(g, (y + k) % 4, 1, keepdims=False), "y", k)

    new_first = 0.9 * first_moment + 0.1 * grad
    new_second = 0.999 * second_moment + 0.001 * grad * grad
    first_fix = 1.0 - 0.9**STEP
    second_fix = 1.0 - 0.999**STEP
    normed = (new_first / first_fix / (jnp.sqrt(new_second / second_fix) + 1e-08)).astype(BF)
    normed_all = gather_rows(gather_rows(normed, "x", x), "zh", zh)
    update = jnp.dot(basis, normed_all, preferred_element_type=F32).astype(BF)

    def slot_of(k):
        dest = (x + k) % 4
        return 2 * ((dest // 2) ^ zl) + ((dest % 2) ^ c)

    order_k = (2, 1, 3, 0)
    pick_x = jnp.stack([slot_of(k) for k in order_k]).astype(jnp.int32)
    pick_z = jnp.stack([(zh + k - y) % 4 for k in order_k]).astype(jnp.int32)
    outs = []
    for start, rows, sets in GROUPS:
        parts = []
        for offsets in sets:
            pieces = partials(hidden, [slots[o] for o in offsets], pick_x, start, rows)
            parts += [pieces[6], *ring("x", *pieces[:6])]
        pieces = regroup(parts, sets, pick_z, rows)
        last_up, near_dn, near_up, last_dn = ring("zh", *pieces[:6])
        own = pieces[6]
        half = rows // 2
        outs.append((own[:half] + last_up.astype(F32) + near_dn.astype(F32)).astype(BF))
        outs.append((own[half:] + near_up.astype(F32) + last_dn.astype(F32)).astype(BF))
    output = jnp.concatenate(outs, axis=0)

    order, shards = [], []
    for off, four in slots.items():
        for slot, w in enumerate(four):
            order.append(((y + off) % 4) * 4 + 2 * (zl ^ (slot // 2)) + (c ^ (slot % 2)))
            shards.append(w)
    act_grad = act(cotangent, shards, jnp.stack(order).astype(jnp.int32))
    return output, act_grad, new_first, new_second, update


def solution(mesh):
    fine = Mesh(mesh.devices.reshape(tuple(SIZE[a] for a in AXES)), AXES)
    dp, fsdp = ("zh", "x"), ("y", "zl", "c")
    in_specs = (
        P(fsdp, dp),
        P(fsdp, None),
        P(dp, fsdp),
        P(dp, None),
        P(dp, fsdp),
        P(dp, fsdp),
    )
    out_specs = (P(fsdp, dp), P(fsdp, dp), P(dp, fsdp), P(dp, fsdp), P(dp, fsdp))
    return jax.shard_map(
        on_device, mesh=fine, in_specs=in_specs, out_specs=out_specs, check_vma=False
    )
```

```python
import functools

import jax
import jax.numpy as jnp
from jax import lax
from jax.experimental import pallas as pl
from jax.experimental.pallas import tpu as pltpu
from jax.sharding import Mesh
from jax.sharding import PartitionSpec as P

STEP = 20
BF = jnp.bfloat16
F32 = jnp.float32
AXES = ("zh", "x", "y", "zl", "c")
SIZE = dict(zh=4, x=4, y=4, zl=2, c=2)
FSDP = ("y", "zl", "c")
COLS = 128
MIB = 1024 * 1024


def shift(array, axis, by):
    n = SIZE[axis]
    return lax.ppermute(array, axis, [(i, (i + by) % n) for i in range(n)])


def partial_kernel(half, pick, h_ref, w0, w1, w2, w3, far_up, far_down, near_up, near_down, acc_up, acc_down, own, wide):
    k = pl.program_id(0)
    for block, w in enumerate((w0, w1, w2, w3)):
        wide[:, block * COLS : (block + 1) * COLS] = w[0]
    top = jnp.dot(h_ref[:half], wide[...], preferred_element_type=F32)
    low = jnp.dot(h_ref[half:], wide[...], preferred_element_type=F32)

    @pl.when(k == 0)
    def _():
        far_up[...] = top.astype(BF)
        far_down[...] = low.astype(BF)

    @pl.when(k == 1)
    def _():
        acc_up[...] = top
        near_up[...] = low.astype(BF)

    @pl.when(k == 2)
    def _():
        near_down[...] = top.astype(BF)
        acc_down[...] = low

    @pl.when(k == 3)
    def _():
        own[:half] = top
        own[half:] = low


def partials(hidden, shards, dests):
    tokens, full = hidden.shape
    half = tokens // 2
    width = 4 * COLS
    small = pltpu.HBM((half, width), BF)
    kept = pltpu.HBM((half, width), F32)
    whole = pltpu.HBM((tokens, width), F32)

    def same(k, s):
        return (0, 0)

    def weight_spec(block):
        return pl.BlockSpec((1, full, COLS), lambda k, s: (4 * block + s[k], 0, 0))

    return pl.pallas_call(
        functools.partial(partial_kernel, half),
        out_shape=[small] * 4 + [kept] * 2 + [whole],
        grid_spec=pltpu.PrefetchScalarGridSpec(
            num_scalar_prefetch=1,
            grid=(4,),
            in_specs=[pl.BlockSpec((tokens, full), same)] + [weight_spec(b) for b in range(4)],
            out_specs=[pl.BlockSpec((half, width), same)] * 6 + [pl.BlockSpec((tokens, width), same)],
            scratch_shapes=[pltpu.VMEM((full, width), BF)],
        ),
        compiler_params=pltpu.CompilerParams(vmem_limit_bytes=24 * MIB),
        cost_estimate=pl.CostEstimate(
            flops=8 * tokens * full * width, bytes_accessed=8 * MIB, transcendentals=0
        ),
        name="partials",
    )(dests, hidden, shards, shards, shards, shards)


def add_kernel(a, b, ra, rb, out_a, out_b):
    out_a[...] = (a[...] + ra[...].astype(F32)).astype(BF)
    out_b[...] = (b[...] + rb[...].astype(F32)).astype(BF)


def add_pair(a, b, ra, rb):
    rows, width = a.shape
    tile = rows // 3
    spec = pl.BlockSpec((tile, width), lambda i: (i, 0))
    return pl.pallas_call(
        add_kernel,
        out_shape=[pltpu.HBM(a.shape, BF)] * 2,
        grid=(3,),
        in_specs=[spec] * 4,
        out_specs=[spec] * 2,
        compiler_params=pltpu.CompilerParams(vmem_limit_bytes=8 * MIB),
        cost_estimate=pl.CostEstimate(flops=2 * a.size, bytes_accessed=16 * a.size, transcendentals=0),
        name="add_pair",
    )(a, b, ra, rb)


def regroup_kernel(pick, own, last_up, near_dn, near_up, last_dn, *outs):
    i = pl.program_id(0)
    mine = own[...]
    first = mine + last_up[...].astype(F32) + near_dn[...].astype(F32)
    second = mine + near_up[...].astype(F32) + last_dn[...].astype(F32)
    own_total = outs[4]
    own_total[...] = jnp.where(i == 0, first, second)
    for k in range(4):
        cols = pl.ds(pl.multiple_of(pick[k] * COLS, COLS), COLS)
        outs[k][...] = own_total[:, cols].astype(outs[k].dtype)


def regroup(own, got, pick):
    rows, width = own.shape
    half = rows // 2
    part = pl.BlockSpec((half, width), lambda i, s: (0, 0))
    return pl.pallas_call(
        regroup_kernel,
        out_shape=[pltpu.HBM((rows, COLS), BF)] * 3 + [pltpu.HBM((rows, COLS), F32)],
        grid_spec=pltpu.PrefetchScalarGridSpec(
            num_scalar_prefetch=1,
            grid=(2,),
            in_specs=[pl.BlockSpec((half, width), lambda i, s: (i, 0))] + [part] * 4,
            out_specs=[pl.BlockSpec((half, COLS), lambda i, s: (i, 0))] * 4,
            scratch_shapes=[pltpu.VMEM((half, width), F32)],
        ),
        compiler_params=pltpu.CompilerParams(vmem_limit_bytes=12 * MIB),
        cost_estimate=pl.CostEstimate(flops=rows * 4096, bytes_accessed=4 * MIB, transcendentals=0),
        name="regroup",
    )(pick, own, *got)


def finish_kernel(*refs):
    out = refs[8]
    for s in range(2):
        own, a, b, c = refs[4 * s : 4 * s + 4]
        total = own[...] + a[...].astype(F32) + b[...].astype(F32) + c[...].astype(F32)
        out[:, s * COLS : (s + 1) * COLS] = total.astype(BF)


def finish(parts):
    rows = parts[0].shape[0]
    tile = rows // 2
    spec = pl.BlockSpec((tile, COLS), lambda i: (i, 0))
    return pl.pallas_call(
        finish_kernel,
        out_shape=jax.ShapeDtypeStruct((rows, 2 * COLS), BF),
        grid=(2,),
        in_specs=[spec] * 8,
        out_specs=pl.BlockSpec((tile, 2 * COLS), lambda i: (i, 0)),
        compiler_params=pltpu.CompilerParams(vmem_limit_bytes=8 * MIB),
        cost_estimate=pl.CostEstimate(flops=rows * 1024, bytes_accessed=2 * MIB, transcendentals=0),
        name="finish",
    )(*parts)


def act_kernel(cot_ref, first, second, out_ref, wide):
    @pl.when(pl.program_id(0) == 0)
    def _():
        for j in range(16):
            wide[:, 256 * j : 256 * j + COLS] = first[j]
            wide[:, 256 * j + COLS : 256 * j + 256] = second[j]

    out_ref[...] = lax.dot_general(
        cot_ref[...], wide[...], (((1,), (1,)), ((), ())), preferred_element_type=F32
    ).astype(BF)


def act(cotangent, first, second):
    tokens, features = cotangent.shape
    tile = 192
    full = first.shape[1]
    spec = pl.BlockSpec((16, full, COLS), lambda i: (0, 0, 0), pipeline_mode=pl.Buffered(1))
    return pl.pallas_call(
        act_kernel,
        out_shape=jax.ShapeDtypeStruct((tokens, full), BF),
        grid=(tokens // tile,),
        in_specs=[pl.BlockSpec((tile, features), lambda i: (i, 0)), spec, spec],
        out_specs=pl.BlockSpec((tile, full), lambda i: (i, 0)),
        scratch_shapes=[pltpu.VMEM((full, features), BF)],
        compiler_params=pltpu.CompilerParams(vmem_limit_bytes=28 * MIB),
        cost_estimate=pl.CostEstimate(
            flops=2 * tokens * features * full, bytes_accessed=16 * MIB, transcendentals=0
        ),
        name="act_grad",
    )(cotangent, first, second)


def place_kernel(at, *refs):
    out = refs[-1]
    rows = refs[0].shape[0]
    for k, piece in enumerate(refs[:-1]):
        start = pl.multiple_of(((at[0] + k) % 4) * rows, rows)
        out[pl.ds(start, rows), :] = piece[...]


def gather_rows(block, axis, at):
    n = SIZE[axis]
    pieces = [block] + [shift(block, axis, -k) for k in range(1, n)]
    rows, width = block.shape
    return pl.pallas_call(
        place_kernel,
        out_shape=jax.ShapeDtypeStruct((n * rows, width), block.dtype),
        in_specs=[pl.BlockSpec(memory_space=pltpu.SMEM)] + [pl.BlockSpec(memory_space=pltpu.VMEM)] * n,
        out_specs=pl.BlockSpec(memory_space=pltpu.VMEM),
        cost_estimate=pl.CostEstimate(flops=0, bytes_accessed=8 * rows * width * 2, transcendentals=0),
        name="place",
    )(at[None].astype(jnp.int32), *pieces)


def after(value, *others):
    return lax.optimization_barrier((value, *others))[0]


def on_device(hidden, cotangent, weight, basis, first_moment, second_moment):
    zh, x, y, zl, c = (lax.axis_index(a) for a in AXES)
    tokens, full = hidden.shape

    shards = [
        lax.all_gather(weight[:, s * COLS : (s + 1) * COLS], FSDP, axis=0, tiled=False) for s in range(2)
    ]

    low_part = lax.dot_general(
        basis, hidden, (((0,), (1,)), ((), ())), preferred_element_type=F32
    ).astype(BF)
    low4 = low_part.reshape(4, 4, 32, tokens)

    def low_to(k):
        return lax.dynamic_index_in_dim(low4, (x + k) % 4, 1, keepdims=False)

    low_x = low_to(0).astype(F32)
    for k in (1, 2, 3):
        low_x = low_x + shift(low_to(k), "x", k).astype(F32)
    low_xb = low_x.astype(BF)

    def low_zto(k):
        return lax.dynamic_index_in_dim(low_xb, (zh + k) % 4, 0, keepdims=False)

    low = lax.dynamic_index_in_dim(low_x, zh, 0, keepdims=False)
    for k in (1, 2, 3):
        low = low + shift(low_zto(k), "zh", k).astype(F32)
    low = low.astype(BF)
    grad_part = jnp.dot(low, cotangent, preferred_element_type=F32)

    dests = jnp.stack([(x + k) % 4 for k in (2, 1, 3, 0)]).astype(jnp.int32)
    dests_z = jnp.stack([(zh + k) % 4 for k in (1, 2, 3, 0)]).astype(jnp.int32)

    def ring_first(pieces):
        far_up, far_down, near_up, near_down, acc_up, acc_down, own = pieces
        got_far = shift(far_up, "x", 1), shift(far_down, "x", -1)
        got_near_up, got_near_down = shift(near_up, "x", 1), shift(near_down, "x", -1)
        return add_pair(acc_up, acc_down, *got_far), (got_near_up, got_near_down)

    def ring_last(last, near):
        return shift(last[0], "x", 1), near[1], near[0], shift(last[1], "x", -1)

    def z_send(pieces):
        return [pieces[3]] + [shift(pieces[k - 1], "zh", k) for k in (1, 2, 3)]

    pieces1 = partials(after(hidden, grad_part), shards[0], dests)
    g = after(grad_part, *pieces1[:4]).reshape(32, 8, 2, 256)
    g = lax.dynamic_index_in_dim(g, c, 2, keepdims=False) + shift(
        lax.dynamic_index_in_dim(g, 1 - c, 2, keepdims=False), "c", 1
    )
    g = g.reshape(32, 4, 2, 256)
    g = lax.dynamic_index_in_dim(g, zl, 2, keepdims=False) + shift(
        lax.dynamic_index_in_dim(g, 1 - zl, 2, keepdims=False), "zl", 1
    )
    last1, near1 = ring_first(pieces1)
    grad = lax.dynamic_index_in_dim(g, y, 1, keepdims=False)
    for k in (1, 2, 3):
        grad = grad + shift(lax.dynamic_index_in_dim(g, (y + k) % 4, 1, keepdims=False), "y", k)
    new_first = 0.9 * first_moment + 0.1 * grad
    new_second = 0.999 * second_moment + 0.001 * grad * grad
    first_fix = 1.0 - 0.9**STEP
    second_fix = 1.0 - 0.999**STEP
    normed = (new_first / first_fix / (jnp.sqrt(new_second / second_fix) + 1e-08)).astype(BF)

    pieces2 = partials(after(hidden, *last1), shards[1], dests)
    normed_x = gather_rows(after(normed, *pieces2[:4]), "x", x)
    got1 = ring_last(last1, near1)
    last2, near2 = ring_first(pieces2)
    zpieces1 = regroup(pieces1[6], got1, dests_z)
    normed_all = gather_rows(after(normed_x, *zpieces1), "zh", zh)
    update = jnp.dot(basis, normed_all, preferred_element_type=F32).astype(BF)
    got2 = ring_last(last2, near2)
    act_grad = act(after(cotangent, *last2, *zpieces1), *shards)
    z1 = z_send(zpieces1)
    zpieces2 = regroup(pieces2[6], got2, dests_z)
    z2 = z_send(zpieces2)
    output = finish(z1 + z2)
    return output, act_grad, new_first, new_second, update


def solution(mesh):
    fine = Mesh(mesh.devices.reshape(tuple(SIZE[a] for a in AXES)), AXES)
    dp = ("zh", "x")
    in_specs = (
        P(FSDP, dp),
        P(FSDP, None),
        P(dp, FSDP),
        P(dp, None),
        P(dp, FSDP),
        P(dp, FSDP),
    )
    out_specs = (P(FSDP, dp), P(FSDP, dp), P(dp, FSDP), P(dp, FSDP), P(dp, FSDP))
    return jax.shard_map(
        on_device, mesh=fine, in_specs=in_specs, out_specs=out_specs, check_vma=False
    )
```

```python
import functools

import jax
import jax.numpy as jnp
from jax import lax
from jax.experimental import pallas as pl
from jax.experimental.pallas import tpu as pltpu
from jax.sharding import Mesh
from jax.sharding import PartitionSpec as P

STEP = 20
BF = jnp.bfloat16
F32 = jnp.float32
AXES = ("zh", "x", "y", "zl", "c")
SIZE = dict(zh=4, x=4, y=4, zl=2, c=2)
FSDP = ("y", "zl", "c")
DP = ("zh", "x")
W = 256
MIB = 1024 * 1024
SMALL = pl.CostEstimate(flops=1 << 20, bytes_accessed=1 << 16, transcendentals=0)


def shift(array, axis, by):
    n = SIZE[axis]
    return lax.ppermute(array, axis, [(i, (i + by) % n) for i in range(n)])


def swap(array, axes):
    return lax.all_to_all(array, axes, 0, 0, tiled=True)


def after(value, *others):
    return lax.optimization_barrier((value, *others))[0]


def in_hbm(value):
    return pltpu.with_memory_space_constraint(value, pltpu.HBM)


def params(limit):
    return pltpu.CompilerParams(vmem_limit_bytes=limit * MIB)


def partial_kernel(m, slot_of, h_ref, *refs):
    w_refs, outs, wide = refs[: 4 * m], refs[4 * m : 4 * m + 4], refs[4 * m + 4]
    k = pl.program_id(0)
    for slot in range(4):

        @pl.when(slot_of[k] == slot)
        def _(slot=slot):
            for block in range(m):
                wide[:, block * W : (block + 1) * W] = w_refs[4 * block + slot][...]

    product = jnp.dot(h_ref[...], wide[...], preferred_element_type=F32).astype(BF)
    for which in range(4):

        @pl.when(k == which)
        def _(which=which):
            outs[which][...] = product


def partials(hidden, blocks, slot_of, start, rows):
    full = hidden.shape[1]
    m = len(blocks)
    flat = [w for four in blocks for w in four]
    return pl.pallas_call(
        functools.partial(partial_kernel, m),
        out_shape=[pltpu.HBM((rows, m * W), BF)] * 4,
        grid_spec=pltpu.PrefetchScalarGridSpec(
            num_scalar_prefetch=1,
            grid=(4,),
            in_specs=[pl.BlockSpec((rows, full), lambda n, s: (start // rows, 0))]
            + [pl.BlockSpec((full, W), lambda n, s: (0, 0), pipeline_mode=pl.Buffered(1))] * (4 * m),
            out_specs=[pl.BlockSpec((rows, m * W), lambda n, s: (0, 0))] * 4,
            scratch_shapes=[pltpu.VMEM((full, m * W), BF)],
        ),
        compiler_params=params(20),
        cost_estimate=SMALL,
        name="partials",
    )(slot_of, in_hbm(hidden), *flat)


def regroup_kernel(offsets, place, *refs):
    out = refs[-1]
    for s, offs in enumerate(offsets):
        four = refs[4 * s : 4 * s + 4]
        total = four[0][...].astype(F32)
        for ref in four[1:]:
            total += ref[...].astype(F32)
        total = total.astype(BF)
        for block, off in enumerate(offs):
            out[place[off]] = total[:, block * W : (block + 1) * W]


def regroup(first, second, offsets, place, start, rows):
    tile = rows // 2
    return pl.pallas_call(
        functools.partial(regroup_kernel, offsets),
        out_shape=pltpu.HBM((4, rows, W), BF),
        grid_spec=pltpu.PrefetchScalarGridSpec(
            num_scalar_prefetch=1,
            grid=(2,),
            in_specs=[pl.BlockSpec((tile, W), lambda i, s: (start // tile + i, 0))] * 4
            + [pl.BlockSpec((tile, 3 * W), lambda i, s: (i, 0))] * 4,
            out_specs=pl.BlockSpec((4, tile, W), lambda i, s: (0, i, 0)),
        ),
        compiler_params=params(16),
        cost_estimate=SMALL,
        name="regroup",
    )(place, *first, *second)


def x_reduce(parts):
    return [parts[3]] + [shift(parts[k - 1], "x", k) for k in (1, 3, 2)]


def finish_kernel(first, second, out):
    i = pl.program_id(0)
    for which, ref in enumerate((first, second)):

        @pl.when(i == which)
        def _(ref=ref):
            total = ref[0].astype(F32)
            for s in range(1, 4):
                total += ref[s].astype(F32)
            out[...] = total.astype(BF)


def finish(first, second):
    rows = first.shape[1]
    spec = pl.BlockSpec((4, rows, W), lambda i: (0, 0, 0))
    return pl.pallas_call(
        finish_kernel,
        out_shape=jax.ShapeDtypeStruct((2 * rows, W), BF),
        grid=(2,),
        in_specs=[spec] * 2,
        out_specs=pl.BlockSpec((rows, W), lambda i: (i, 0)),
        compiler_params=params(12),
        cost_estimate=SMALL,
        name="finish",
    )(first, second)


def act_kernel(order, cot_ref, *refs):
    w_refs, out_ref, wide = refs[:16], refs[16], refs[17]

    @pl.when(pl.program_id(0) == 0)
    def _():
        for s in range(16):
            wide[:, pl.ds(pl.multiple_of(order[s] * W, W), W)] = w_refs[s][...]

    out_ref[...] = lax.dot_general(
        cot_ref[...], wide[...], (((1,), (1,)), ((), ())), preferred_element_type=F32
    ).astype(BF)


def act(cotangent, shards, order):
    tokens, features = cotangent.shape
    tile = tokens // 2
    full = shards[0].shape[0]
    spec = pl.BlockSpec((full, W), lambda i, s: (0, 0), pipeline_mode=pl.Buffered(1))
    return pl.pallas_call(
        act_kernel,
        out_shape=jax.ShapeDtypeStruct((tokens, full), BF),
        grid_spec=pltpu.PrefetchScalarGridSpec(
            num_scalar_prefetch=1,
            grid=(tokens // tile,),
            in_specs=[pl.BlockSpec((tile, features), lambda i, s: (i, 0))] + [spec] * 16,
            out_specs=pl.BlockSpec((tile, full), lambda i, s: (i, 0)),
            scratch_shapes=[pltpu.VMEM((full, features), BF)],
        ),
        compiler_params=params(32),
        cost_estimate=SMALL,
        name="act_grad",
    )(order, in_hbm(cotangent), *shards)


def on_device(hidden, cotangent, weight, basis, first_moment, second_moment):
    zh, x, y, zl, c = (lax.axis_index(a) for a in AXES)
    tokens = hidden.shape[0]
    half = tokens // 2

    side = shift(weight, "zl", 1)
    next0, prev0 = shift(weight, "y", -1), shift(weight, "y", 1)
    next1, prev1 = shift(side, "y", -1), shift(side, "y", 1)
    far0 = shift(after(next0, next1), "y", -1)
    far1 = shift(prev1, "y", 1)
    held = {0: (weight, side), 1: (next0, next1), 3: (prev0, prev1), 2: (far0, far1)}
    slots = {
        off: (own, shift(own, "c", 1), other, shift(other, "c", 1)) for off, (own, other) in held.items()
    }
    dest = [2 * (zl ^ (s // 2)) + (c ^ (s % 2)) for s in range(4)]
    goals = [(x + k) % 4 for k in (1, 2, 3, 0)]
    slot_of = jnp.stack([2 * ((g // 2) ^ zl) + ((g % 2) ^ c) for g in goals]).astype(jnp.int32)
    place = jnp.stack([(y + k) % 4 for k in range(4)]).astype(jnp.int32)

    low_part = lax.dot_general(
        basis, hidden, (((0,), (1,)), ((), ())), preferred_element_type=F32
    ).astype(BF)
    low_all = swap(low_part.reshape(16, 32, tokens), DP)

    part0 = partials(after(hidden, next0, prev0), [slots[0]], slot_of, 0, tokens)
    sum0 = x_reduce(part0)

    low = jnp.sum(after(low_all, *part0).astype(F32), axis=0).astype(BF)
    grad_part = jnp.dot(low, cotangent, preferred_element_type=F32)
    grad_all = swap(grad_part.reshape(32, 16, W).transpose(1, 0, 2), FSDP)

    others = (1, 3, 2)
    kept = {off: [in_hbm(w) for w in four] for off, four in slots.items()}
    rest = [kept[off] for off in others]
    part1 = partials(after(hidden, grad_part, *sum0[1:]), rest, slot_of, 0, half)
    sum1 = x_reduce(part1)

    grad = jnp.sum(after(grad_all, *part1), axis=0)
    new_first = 0.9 * first_moment + 0.1 * grad
    new_second = 0.999 * second_moment + 0.001 * grad * grad
    first_fix = 1.0 - 0.9**STEP
    second_fix = 1.0 - 0.999**STEP
    normed = (new_first / first_fix / (jnp.sqrt(new_second / second_fix) + 1e-08)).astype(BF)
    normed_all = swap(jnp.broadcast_to(normed[None], (16, *normed.shape)), DP)

    part2 = partials(after(hidden, *part1), rest, slot_of, half, half)
    sum2 = x_reduce(lax.optimization_barrier((*part2, *sum1[1:]))[:4])

    order, shards = [], []
    for off, four in kept.items():
        for slot, w in enumerate(four):
            order.append(((y + off) % 4) * 4 + dest[slot])
            shards.append(w)
    act_grad = act(after(cotangent, *part2), shards, jnp.stack(order).astype(jnp.int32))
    offsets = ((0,), others)
    zpart1 = regroup(sum0, sum1, offsets, after(place, act_grad, *part2), 0, half)
    normed_all = after(normed_all, zpart1).reshape(-1, W)
    update = jnp.dot(basis, normed_all, preferred_element_type=F32).astype(BF)
    got1 = swap(zpart1, "zh")
    got2 = swap(regroup(sum0, sum2, offsets, place, half, half), "zh")
    output = finish(got1, got2)
    return output, act_grad, new_first, new_second, update


def solution(mesh):
    fine = Mesh(mesh.devices.reshape(tuple(SIZE[a] for a in AXES)), AXES)
    in_specs = (
        P(FSDP, DP),
        P(FSDP, None),
        P(DP, FSDP),
        P(DP, None),
        P(DP, FSDP),
        P(DP, FSDP),
    )
    out_specs = (P(FSDP, DP), P(FSDP, DP), P(DP, FSDP), P(DP, FSDP), P(DP, FSDP))
    return jax.shard_map(
        on_device, mesh=fine, in_specs=in_specs, out_specs=out_specs, check_vma=False
    )
```

```python
import functools

import jax
import jax.numpy as jnp
from jax import lax
from jax.experimental import pallas as pl
from jax.experimental.pallas import tpu as pltpu
from jax.sharding import Mesh
from jax.sharding import PartitionSpec as P

STEP = 20
BF = jnp.bfloat16
F32 = jnp.float32
AXES = ("zh", "x", "y", "zl", "c")
SIZE = dict(zh=4, x=4, y=4, zl=2, c=2)
FSDP = ("y", "zl", "c")
DP = ("zh", "x")
W = 256
MIB = 1024 * 1024
LIGHT = pl.CostEstimate(flops=1 << 20, bytes_accessed=1 << 16, transcendentals=0)
COST = pl.CostEstimate(flops=1 << 33, bytes_accessed=1 << 25, transcendentals=0)


def shift(array, axis, by):
    n = SIZE[axis]
    return lax.ppermute(array, axis, [(i, (i + by) % n) for i in range(n)])


def swap(array, axes):
    return lax.all_to_all(array, axes, 0, 0, tiled=True)


def after(value, *others):
    return lax.optimization_barrier((value, *others))[0]


def in_hbm(value):
    return pltpu.with_memory_space_constraint(value, pltpu.HBM)


def params(limit):
    return pltpu.CompilerParams(vmem_limit_bytes=limit * MIB)


def partial_kernel(m, slot_of, h_ref, *refs):
    w_refs, outs = refs[: 4 * m], refs[4 * m : 4 * m + 4]
    wide, held, w_sems, out_sems = refs[4 * m + 4 :]

    def fetch(k):
        for block in range(m):
            for slot in range(4):

                @pl.when(slot_of[k] == slot)
                def _(block=block, slot=slot):
                    load(k, block, slot).start()

    def load(k, block, slot):
        return pltpu.make_async_copy(
            w_refs[4 * block + slot],
            wide.at[k % 2, :, pl.ds(block * W, W)],
            w_sems.at[k % 2, block],
        )

    def store(k):
        return pltpu.make_async_copy(held.at[k % 2], outs[k], out_sems.at[k % 2])

    fetch(0)
    fetch(1)
    for k in range(4):
        for block in range(m):
            load(k, block, 0).wait()
        if k >= 2:
            store(k - 2).wait()
        held[k % 2] = jnp.dot(h_ref[...], wide[k % 2], preferred_element_type=F32).astype(BF)
        store(k).start()
        if k < 2:
            fetch(k + 2)
    store(2).wait()
    store(3).wait()


def partials(hidden, blocks, slot_of, start, rows):
    full = hidden.shape[1]
    m = len(blocks)
    flat = [w for four in blocks for w in four]
    return pl.pallas_call(
        functools.partial(partial_kernel, m),
        out_shape=[pltpu.HBM((rows, m * W), BF)] * 4,
        grid_spec=pltpu.PrefetchScalarGridSpec(
            num_scalar_prefetch=1,
            grid=(1,),
            in_specs=[pl.BlockSpec((rows, full), lambda n, s: (start // rows, 0))]
            + [pl.BlockSpec(memory_space=pl.ANY)] * (4 * m),
            out_specs=[pl.BlockSpec(memory_space=pl.ANY)] * 4,
            scratch_shapes=[
                pltpu.VMEM((2, full, m * W), BF),
                pltpu.VMEM((2, rows, m * W), BF),
                pltpu.SemaphoreType.DMA((2, m)),
                pltpu.SemaphoreType.DMA((2,)),
            ],
        ),
        compiler_params=params(14),
        cost_estimate=COST,
        name="partials",
    )(slot_of, in_hbm(hidden), *flat)


def regroup_kernel(offsets, place, *refs):
    outs = refs[8:]
    for s, offs in enumerate(offsets):
        four = refs[4 * s : 4 * s + 4]
        total = four[0][...].astype(F32)
        for ref in four[1:]:
            total += ref[...].astype(F32)
        total = total.astype(BF)
        for block, off in enumerate(offs):
            for which in range(4):

                @pl.when(place[off] == which)
                def _(total=total, block=block, which=which):
                    outs[which][...] = total[:, block * W : (block + 1) * W]


def regroup(first, second, offsets, place, start, rows):
    tile = rows // 2
    return pl.pallas_call(
        functools.partial(regroup_kernel, offsets),
        out_shape=[pltpu.HBM((rows, W), BF)] * 4,
        grid_spec=pltpu.PrefetchScalarGridSpec(
            num_scalar_prefetch=1,
            grid=(2,),
            in_specs=[pl.BlockSpec((tile, W), lambda i, s: (start // tile + i, 0))] * 4
            + [pl.BlockSpec((tile, 3 * W), lambda i, s: (i, 0))] * 4,
            out_specs=[pl.BlockSpec((tile, W), lambda i, s: (i, 0))] * 4,
        ),
        compiler_params=params(16),
        cost_estimate=COST,
        name="regroup",
    )(place, *first, *second)


def spread(parts, axis):
    got = [parts[3]] + [shift(parts[k - 1], axis, k) for k in (1, 3, 2)]
    return [in_hbm(part) for part in got] if axis == "x" else got


def finish_kernel(*refs):
    i = pl.program_id(0)
    out = refs[8]
    for which in range(2):

        @pl.when(i == which)
        def _(which=which):
            four = refs[4 * which : 4 * which + 4]
            total = four[0][...].astype(F32)
            for ref in four[1:]:
                total += ref[...].astype(F32)
            out[...] = total.astype(BF)


def finish(first, second):
    rows = first[0].shape[0]
    spec = pl.BlockSpec((rows, W), lambda i: (0, 0))
    return pl.pallas_call(
        finish_kernel,
        out_shape=jax.ShapeDtypeStruct((2 * rows, W), BF),
        grid=(2,),
        in_specs=[spec] * 8,
        out_specs=pl.BlockSpec((rows, W), lambda i: (i, 0)),
        compiler_params=params(12),
        cost_estimate=LIGHT,
        name="finish",
    )(*first, *second)


def low_kernel(parts, out):
    total = parts[0].astype(F32)
    for s in range(1, 4):
        total += parts[s].astype(F32)
    out[...] = total.astype(BF)


def low_sum(parts):
    return pl.pallas_call(
        low_kernel,
        out_shape=jax.ShapeDtypeStruct(parts.shape[1:], BF),
        in_specs=[pl.BlockSpec(memory_space=pltpu.VMEM)],
        out_specs=pl.BlockSpec(memory_space=pltpu.VMEM),
        compiler_params=params(8),
        cost_estimate=COST,
        name="low_sum",
    )(parts)


def grad_kernel(low_ref, cot_ref, out, low):
    @pl.when(pl.program_id(0) == 0)
    def _():
        low_kernel(low_ref, low)

    for block in range(4):
        out[block] = jnp.dot(
            low[...], cot_ref[:, block * W : (block + 1) * W], preferred_element_type=F32
        )


def grad_partial(low_parts, cotangent):
    tokens, features = cotangent.shape
    ranks = low_parts.shape[1]
    return pl.pallas_call(
        grad_kernel,
        out_shape=pltpu.HBM((features // W, ranks, W), F32),
        grid=(features // (4 * W),),
        in_specs=[
            pl.BlockSpec(low_parts.shape, lambda i: (0, 0, 0)),
            pl.BlockSpec((tokens, 4 * W), lambda i: (0, i)),
        ],
        out_specs=pl.BlockSpec((4, ranks, W), lambda i: (i, 0, 0)),
        scratch_shapes=[pltpu.VMEM((ranks, tokens), BF)],
        compiler_params=params(8),
        cost_estimate=COST,
        name="grad_partial",
    )(low_parts, in_hbm(cotangent))


def moments_kernel(grads, first, second, new_first, new_second, normed):
    grad = grads[0]
    for s in range(1, 16):
        grad = grad + grads[s]
    one = 0.9 * first[...] + 0.1 * grad
    two = 0.999 * second[...] + 0.001 * grad * grad
    new_first[...] = one
    new_second[...] = two
    first_fix = 1.0 - 0.9**STEP
    second_fix = 1.0 - 0.999**STEP
    step = (one / first_fix / (jnp.sqrt(two / second_fix) + 1e-08)).astype(BF)
    for s in range(16):
        normed[s] = step


def moments(grads, first, second):
    full = pl.BlockSpec(memory_space=pltpu.VMEM)
    return pl.pallas_call(
        moments_kernel,
        out_shape=[jax.ShapeDtypeStruct(first.shape, F32)] * 2
        + [jax.ShapeDtypeStruct((16, *first.shape), BF)],
        in_specs=[full] * 3,
        out_specs=[full] * 3,
        compiler_params=params(8),
        cost_estimate=LIGHT,
        name="moments",
    )(grads, first, second)


def act_kernel(order, cot_ref, *refs):
    w_refs, out_ref, wide = refs[:16], refs[16], refs[17]

    @pl.when(pl.program_id(0) == 0)
    def _():
        for s in range(16):
            wide[:, pl.ds(pl.multiple_of(order[s] * W, W), W)] = w_refs[s][...]

    out_ref[...] = lax.dot_general(
        cot_ref[...], wide[...], (((1,), (1,)), ((), ())), preferred_element_type=F32
    ).astype(BF)


def act(cotangent, shards, order):
    tokens, features = cotangent.shape
    tile = tokens // 2
    full = shards[0].shape[0]
    spec = pl.BlockSpec((full, W), lambda i, s: (0, 0), pipeline_mode=pl.Buffered(1))
    return pl.pallas_call(
        act_kernel,
        out_shape=jax.ShapeDtypeStruct((tokens, full), BF),
        grid_spec=pltpu.PrefetchScalarGridSpec(
            num_scalar_prefetch=1,
            grid=(tokens // tile,),
            in_specs=[pl.BlockSpec((tile, features), lambda i, s: (i, 0))] + [spec] * 16,
            out_specs=pl.BlockSpec((tile, full), lambda i, s: (i, 0)),
            scratch_shapes=[pltpu.VMEM((full, features), BF)],
        ),
        compiler_params=params(32),
        cost_estimate=COST,
        name="act_grad",
    )(order, in_hbm(cotangent), *shards)


def on_device(hidden, cotangent, weight, basis, first_moment, second_moment):
    zh, x, y, zl, c = (lax.axis_index(a) for a in AXES)
    tokens = hidden.shape[0]
    half = tokens // 2

    low_part = lax.dot_general(
        basis, hidden, (((0,), (1,)), ((), ())), preferred_element_type=F32
    ).astype(BF)
    low_part = low_part.reshape(4, 4, 32, tokens).transpose(1, 0, 2, 3)

    side = shift(weight, "zl", 1)
    next0, prev0 = shift(weight, "y", -1), shift(weight, "y", 1)
    low_x = swap(after(low_part, weight), "x")
    side = after(side, low_part, next0, prev0)
    next1, prev1 = shift(side, "y", -1), shift(side, "y", 1)

    def both_cores(own, other):
        return own, shift(own, "c", 1), other, shift(other, "c", 1)

    dest = [2 * (zl ^ (s // 2)) + (c ^ (s % 2)) for s in range(4)]
    goals = [(x + k) % 4 for k in (1, 2, 3, 0)]
    slot_of = jnp.stack([2 * ((g // 2) ^ zl) + ((g % 2) ^ c) for g in goals]).astype(jnp.int32)
    place = jnp.stack([(y + k - zh + 3) % 4 for k in range(4)]).astype(jnp.int32)

    slots = {0: both_cores(weight, side)}
    part0 = partials(after(hidden, next0, prev0, low_x), [slots[0]], slot_of, 0, tokens)
    sum0 = spread(part0, "x")
    far0 = shift(after(next0, next1, *part0), "y", -1)
    far1 = shift(after(prev1, *part0), "y", 1)
    slots[1] = both_cores(next0, next1)
    slots[3] = both_cores(prev0, prev1)
    slots[2] = both_cores(after(far0, *sum0[1:]), after(far1, *sum0[1:]))

    low_x = low_sum(after(low_x, *part0))
    low_z = swap(low_x, "zh")

    others = (1, 3, 2)
    kept = {off: [in_hbm(w) for w in four] for off, four in slots.items()}
    rest = [kept[off] for off in others]
    part1 = partials(after(hidden, low_x), rest, slot_of, 0, half)
    sum1 = spread(part1, "x")

    part2 = partials(after(hidden, *part1), rest, slot_of, half, half)
    grad_all = swap(grad_partial(after(low_z, *part2), cotangent), FSDP)

    sum2 = spread(lax.optimization_barrier((*part2, *sum1[1:]))[:4], "x")
    offsets = ((0,), others)
    zpart1 = regroup(sum0, sum1, offsets, after(place, *part2), 0, half)
    got1 = spread(zpart1, "zh")

    new_first, new_second, normed = moments(after(grad_all, *zpart1), first_moment, second_moment)
    normed_all = swap(normed, DP)

    order, shards = [], []
    for off, four in kept.items():
        for slot, w in enumerate(four):
            order.append(((y + off) % 4) * 4 + dest[slot])
            shards.append(w)
    zpart2 = regroup(sum0, sum2, offsets, after(place, *zpart1), half, half)
    got2 = spread(zpart2, "zh")
    act_grad = act(after(cotangent, *zpart2), shards, jnp.stack(order).astype(jnp.int32))
    normed_all = after(normed_all, *zpart2).reshape(-1, W)
    update = jnp.dot(basis, normed_all, preferred_element_type=F32).astype(BF)
    output = finish(got1, got2)
    return output, act_grad, new_first, new_second, update


def solution(mesh):
    fine = Mesh(mesh.devices.reshape(tuple(SIZE[a] for a in AXES)), AXES)
    in_specs = (
        P(FSDP, DP),
        P(FSDP, None),
        P(DP, FSDP),
        P(DP, None),
        P(DP, FSDP),
        P(DP, FSDP),
    )
    out_specs = (P(FSDP, DP), P(FSDP, DP), P(DP, FSDP), P(DP, FSDP), P(DP, FSDP))
    return jax.shard_map(
        on_device, mesh=fine, in_specs=in_specs, out_specs=out_specs, check_vma=False
    )
```

```python
import functools

import jax
import jax.numpy as jnp
from jax import lax
from jax.experimental import pallas as pl
from jax.experimental.pallas import tpu as pltpu
from jax.sharding import Mesh
from jax.sharding import PartitionSpec as P

STEP = 20
BF = jnp.bfloat16
F32 = jnp.float32
AXES = ("zh", "x", "y", "zl", "c")
SIZE = dict(zh=4, x=4, y=4, zl=2, c=2)
FSDP = ("y", "zl", "c")
DP = ("zh", "x")
W = 256
MIB = 1024 * 1024
LIGHT = pl.CostEstimate(flops=1 << 20, bytes_accessed=1 << 16, transcendentals=0)
COST = pl.CostEstimate(flops=1 << 33, bytes_accessed=1 << 25, transcendentals=0)


def shift(array, axis, by):
    n = SIZE[axis]
    return lax.ppermute(array, axis, [(i, (i + by) % n) for i in range(n)])


def swap(array, axes):
    return lax.all_to_all(array, axes, 0, 0, tiled=True)


def after(value, *others):
    return lax.optimization_barrier((value, *others))[0]


def in_hbm(value):
    return pltpu.with_memory_space_constraint(value, pltpu.HBM)


def params(limit):
    return pltpu.CompilerParams(vmem_limit_bytes=limit * MIB)


def partial_kernel(m, slot_of, h_ref, *refs):
    w_refs, outs = refs[: 4 * m], refs[4 * m : 4 * m + 4]
    wide, held, w_sems, out_sems = refs[4 * m + 4 :]

    def fetch(k):
        for block in range(m):
            for slot in range(4):

                @pl.when(slot_of[k] == slot)
                def _(block=block, slot=slot):
                    load(k, block, slot).start()

    def load(k, block, slot):
        return pltpu.make_async_copy(
            w_refs[4 * block + slot],
            wide.at[k % 2, :, pl.ds(block * W, W)],
            w_sems.at[k % 2, block],
        )

    def store(k):
        return pltpu.make_async_copy(held.at[k % 2], outs[k], out_sems.at[k % 2])

    fetch(0)
    fetch(1)
    for k in range(4):
        for block in range(m):
            load(k, block, 0).wait()
        if k >= 2:
            store(k - 2).wait()
        held[k % 2] = jnp.dot(h_ref[...], wide[k % 2], preferred_element_type=F32).astype(BF)
        store(k).start()
        if k < 2:
            fetch(k + 2)
    store(2).wait()
    store(3).wait()


def partials(hidden, blocks, slot_of, start, rows):
    full = hidden.shape[1]
    m = len(blocks)
    flat = [w for four in blocks for w in four]
    return pl.pallas_call(
        functools.partial(partial_kernel, m),
        out_shape=[pltpu.HBM((rows, m * W), BF)] * 4,
        grid_spec=pltpu.PrefetchScalarGridSpec(
            num_scalar_prefetch=1,
            grid=(1,),
            in_specs=[pl.BlockSpec((rows, full), lambda n, s: (start // rows, 0))]
            + [pl.BlockSpec(memory_space=pl.ANY)] * (4 * m),
            out_specs=[pl.BlockSpec(memory_space=pl.ANY)] * 4,
            scratch_shapes=[
                pltpu.VMEM((2, full, m * W), BF),
                pltpu.VMEM((2, rows, m * W), BF),
                pltpu.SemaphoreType.DMA((2, m)),
                pltpu.SemaphoreType.DMA((2,)),
            ],
        ),
        compiler_params=params(14),
        cost_estimate=COST,
        name="partials",
    )(slot_of, in_hbm(hidden), *flat)


def regroup_kernel(offsets, place, *refs):
    outs = refs[4 * len(offsets) :]
    for s, offs in enumerate(offsets):
        four = refs[4 * s : 4 * s + 4]
        total = four[0][...].astype(F32)
        for ref in four[1:]:
            total += ref[...].astype(F32)
        total = total.astype(BF)
        for block, off in enumerate(offs):
            for which in range(4):

                @pl.when(place[off] == which)
                def _(total=total, block=block, which=which):
                    outs[which][...] = total[:, block * W : (block + 1) * W]


def regroup(groups, place, start, rows):
    tile = rows // 2
    specs, arrays = [], []
    for four, offs in groups:
        first = start // tile if four[0].shape[0] > rows else 0
        spec = pl.BlockSpec((tile, len(offs) * W), lambda i, s, first=first: (first + i, 0))
        specs += [spec] * 4
        arrays += four
    return pl.pallas_call(
        functools.partial(regroup_kernel, [offs for _, offs in groups]),
        out_shape=[pltpu.HBM((rows, W), BF)] * 4,
        grid_spec=pltpu.PrefetchScalarGridSpec(
            num_scalar_prefetch=1,
            grid=(2,),
            in_specs=specs,
            out_specs=[pl.BlockSpec((tile, W), lambda i, s: (i, 0))] * 4,
        ),
        compiler_params=params(16),
        cost_estimate=COST,
        name="regroup",
    )(place, *arrays)


def spread(parts, axis):
    got = [parts[3]] + [shift(parts[k - 1], axis, k) for k in (1, 3, 2)]
    return [in_hbm(part) for part in got] if axis == "x" else got


def finish_kernel(*refs):
    i = pl.program_id(0)
    out = refs[8]
    for which in range(2):

        @pl.when(i == which)
        def _(which=which):
            four = refs[4 * which : 4 * which + 4]
            total = four[0][...].astype(F32)
            for ref in four[1:]:
                total += ref[...].astype(F32)
            out[...] = total.astype(BF)


def finish(first, second):
    rows = first[0].shape[0]
    spec = pl.BlockSpec((rows, W), lambda i: (0, 0))
    return pl.pallas_call(
        finish_kernel,
        out_shape=jax.ShapeDtypeStruct((2 * rows, W), BF),
        grid=(2,),
        in_specs=[spec] * 8,
        out_specs=pl.BlockSpec((rows, W), lambda i: (i, 0)),
        compiler_params=params(12),
        cost_estimate=LIGHT,
        name="finish",
    )(*first, *second)


def low_kernel(parts, out):
    total = parts[0].astype(F32)
    for s in range(1, 4):
        total += parts[s].astype(F32)
    out[...] = total.astype(BF)


def low_sum(parts):
    return pl.pallas_call(
        low_kernel,
        out_shape=jax.ShapeDtypeStruct(parts.shape[1:], BF),
        in_specs=[pl.BlockSpec(memory_space=pltpu.VMEM)],
        out_specs=pl.BlockSpec(memory_space=pltpu.VMEM),
        compiler_params=params(8),
        cost_estimate=COST,
        name="low_sum",
    )(parts)


def grad_kernel(low_ref, cot_ref, out, low):
    @pl.when(pl.program_id(0) == 0)
    def _():
        low_kernel(low_ref, low)

    for block in range(4):
        out[block] = jnp.dot(
            low[...], cot_ref[:, block * W : (block + 1) * W], preferred_element_type=F32
        )


def grad_partial(low_parts, cotangent):
    tokens, features = cotangent.shape
    ranks = low_parts.shape[1]
    return pl.pallas_call(
        grad_kernel,
        out_shape=pltpu.HBM((features // W, ranks, W), F32),
        grid=(features // (4 * W),),
        in_specs=[
            pl.BlockSpec(low_parts.shape, lambda i: (0, 0, 0)),
            pl.BlockSpec((tokens, 4 * W), lambda i: (0, i)),
        ],
        out_specs=pl.BlockSpec((4, ranks, W), lambda i: (i, 0, 0)),
        scratch_shapes=[pltpu.VMEM((ranks, tokens), BF)],
        compiler_params=params(8),
        cost_estimate=COST,
        name="grad_partial",
    )(low_parts, in_hbm(cotangent))


def moments_kernel(grads, first, second, new_first, new_second, normed):
    grad = grads[0]
    for s in range(1, 16):
        grad = grad + grads[s]
    one = 0.9 * first[...] + 0.1 * grad
    two = 0.999 * second[...] + 0.001 * grad * grad
    new_first[...] = one
    new_second[...] = two
    first_fix = 1.0 - 0.9**STEP
    second_fix = 1.0 - 0.999**STEP
    step = (one / first_fix / (jnp.sqrt(two / second_fix) + 1e-08)).astype(BF)
    for s in range(16):
        normed[s] = step


def moments(grads, first, second):
    full = pl.BlockSpec(memory_space=pltpu.VMEM)
    return pl.pallas_call(
        moments_kernel,
        out_shape=[jax.ShapeDtypeStruct(first.shape, F32)] * 2
        + [jax.ShapeDtypeStruct((16, *first.shape), BF)],
        in_specs=[full] * 3,
        out_specs=[full] * 3,
        compiler_params=params(8),
        cost_estimate=LIGHT,
        name="moments",
    )(grads, first, second)


def act_kernel(order, cot_ref, *refs):
    w_refs, out_ref, wide = refs[:16], refs[16], refs[17]

    @pl.when(pl.program_id(0) == 0)
    def _():
        for s in range(16):
            wide[:, pl.ds(pl.multiple_of(order[s] * W, W), W)] = w_refs[s][...]

    out_ref[...] = lax.dot_general(
        cot_ref[...], wide[...], (((1,), (1,)), ((), ())), preferred_element_type=F32
    ).astype(BF)


def act(cotangent, shards, order):
    tokens, features = cotangent.shape
    tile = tokens // 2
    full = shards[0].shape[0]
    spec = pl.BlockSpec((full, W), lambda i, s: (0, 0), pipeline_mode=pl.Buffered(1))
    return pl.pallas_call(
        act_kernel,
        out_shape=jax.ShapeDtypeStruct((tokens, full), BF),
        grid_spec=pltpu.PrefetchScalarGridSpec(
            num_scalar_prefetch=1,
            grid=(tokens // tile,),
            in_specs=[pl.BlockSpec((tile, features), lambda i, s: (i, 0))] + [spec] * 16,
            out_specs=pl.BlockSpec((tile, full), lambda i, s: (i, 0)),
            scratch_shapes=[pltpu.VMEM((full, features), BF)],
        ),
        compiler_params=params(32),
        cost_estimate=COST,
        name="act_grad",
    )(order, in_hbm(cotangent), *shards)


def on_device(hidden, cotangent, weight, basis, first_moment, second_moment):
    zh, x, y, zl, c = (lax.axis_index(a) for a in AXES)
    tokens = hidden.shape[0]
    half = tokens // 2

    low_part = lax.dot_general(
        basis, hidden, (((0,), (1,)), ((), ())), preferred_element_type=F32
    ).astype(BF)
    low_part = low_part.reshape(4, 4, 32, tokens).transpose(1, 0, 2, 3)

    side = shift(weight, "zl", 1)
    next0, prev0 = shift(weight, "y", -1), shift(weight, "y", 1)
    low_x = swap(after(low_part, weight), "x")
    side = after(side, low_part, next0, prev0)
    next1, prev1 = shift(side, "y", -1), shift(side, "y", 1)

    def both_cores(own, other):
        return own, shift(own, "c", 1), other, shift(other, "c", 1)

    dest = [2 * (zl ^ (s // 2)) + (c ^ (s % 2)) for s in range(4)]
    goals = [(x + k) % 4 for k in (1, 2, 3, 0)]
    slot_of = jnp.stack([2 * ((g // 2) ^ zl) + ((g % 2) ^ c) for g in goals]).astype(jnp.int32)
    place = jnp.stack([(y + k - zh + 3) % 4 for k in range(4)]).astype(jnp.int32)

    slots = {0: both_cores(weight, side)}
    next0c, prev0c = shift(after(next0, low_part), "c", 1), shift(after(prev0, low_part), "c", 1)
    part0 = partials(after(hidden, next0c, prev0c, low_x), [slots[0]], slot_of, 0, tokens)
    sum0 = spread(part0, "x")
    next1c, prev1c = shift(after(next1, *part0), "c", 1), shift(after(prev1, *part0), "c", 1)
    slots[1] = next0, next0c, next1, next1c
    slots[3] = prev0, prev0c, prev1, prev1c
    far0 = shift(after(next0, next1c, prev1c, *part0), "y", -1)
    far1 = shift(after(prev1, next1c, prev1c, *part0), "y", 1)
    slots[2] = both_cores(after(far0, *sum0[1:]), after(far1, *sum0[1:]))
    kept = {off: [in_hbm(w) for w in four] for off, four in slots.items()}

    part1 = partials(after(hidden, *part0), [kept[1], kept[3]], slot_of, 0, half)
    sum1 = spread(part1, "x")
    part_far = partials(after(hidden, *part1), [kept[2]], slot_of, 0, half)
    sum_far = spread(part_far, "x")

    low_z = swap(low_sum(after(low_x, *part1)), "zh")
    others = (1, 3, 2)
    part2 = partials(
        after(hidden, low_z, *sum1[1:], *part_far), [kept[off] for off in others], slot_of, half, half
    )
    sum2 = spread(part2, "x")
    zpart1 = regroup(
        [(sum0, (0,)), (sum1, (1, 3)), (sum_far, (2,))], after(place, *part2), 0, half
    )
    got1 = spread(zpart1, "zh")
    grad_all = swap(grad_partial(after(low_z, *part2), cotangent), FSDP)

    new_first, new_second, normed = moments(after(grad_all, *zpart1), first_moment, second_moment)
    normed_all = swap(normed, DP)

    order, shards = [], []
    for off, four in kept.items():
        for slot, w in enumerate(four):
            order.append(((y + off) % 4) * 4 + dest[slot])
            shards.append(w)
    zpart2 = regroup([(sum0, (0,)), (sum2, others)], after(place, *zpart1), half, half)
    got2 = spread(zpart2, "zh")
    act_grad = act(after(cotangent, *zpart2), shards, jnp.stack(order).astype(jnp.int32))
    normed_all = after(normed_all, *zpart2).reshape(-1, W)
    update = jnp.dot(basis, normed_all, preferred_element_type=F32).astype(BF)
    output = finish(got1, got2)
    return output, act_grad, new_first, new_second, update


def solution(mesh):
    fine = Mesh(mesh.devices.reshape(tuple(SIZE[a] for a in AXES)), AXES)
    in_specs = (
        P(FSDP, DP),
        P(FSDP, None),
        P(DP, FSDP),
        P(DP, None),
        P(DP, FSDP),
        P(DP, FSDP),
    )
    out_specs = (P(FSDP, DP), P(FSDP, DP), P(DP, FSDP), P(DP, FSDP), P(DP, FSDP))
    return jax.shard_map(
        on_device, mesh=fine, in_specs=in_specs, out_specs=out_specs, check_vma=False
    )
```

```python
import functools

import jax
import jax.numpy as jnp
from jax import lax
from jax.experimental import pallas as pl
from jax.experimental.pallas import tpu as pltpu
from jax.sharding import Mesh
from jax.sharding import PartitionSpec as P

STEP = 20
BF = jnp.bfloat16
F32 = jnp.float32
AXES = ("zh", "x", "y", "zl", "c")
SIZE = dict(zh=4, x=4, y=4, zl=2, c=2)
FSDP = ("y", "zl", "c")
DP = ("zh", "x")
W = 256
MIB = 1024 * 1024
LIGHT = pl.CostEstimate(flops=1 << 20, bytes_accessed=1 << 16, transcendentals=0)
COST = pl.CostEstimate(flops=1 << 33, bytes_accessed=1 << 25, transcendentals=0)


def shift(array, axis, by):
    n = SIZE[axis]
    return lax.ppermute(array, axis, [(i, (i + by) % n) for i in range(n)])


def swap(array, axes):
    return lax.all_to_all(array, axes, 0, 0, tiled=True)


def after(value, *others):
    return lax.optimization_barrier((value, *others))[0]


def in_hbm(value):
    return pltpu.with_memory_space_constraint(value, pltpu.HBM)


def params(limit):
    return pltpu.CompilerParams(vmem_limit_bytes=limit * MIB)


def partial_kernel(m, start, slot_of, h_ref, *refs):
    w_refs, outs = refs[: 4 * m], refs[4 * m : 4 * m + 4]
    mine, wide, held, h_sem, w_sems, out_sems = refs[4 * m + 4 :]

    def load(k, block, slot):
        return pltpu.make_async_copy(
            w_refs[4 * block + slot], wide.at[k, :, pl.ds(block * W, W)], w_sems.at[k, block]
        )

    def store(k):
        return pltpu.make_async_copy(held.at[k], outs[k], out_sems.at[k])

    hidden = pltpu.make_async_copy(h_ref.at[pl.ds(start, mine.shape[0])], mine, h_sem)
    hidden.start()
    for k in range(4):
        for block in range(m):
            for slot in range(4):

                @pl.when(slot_of[k] == slot)
                def _(k=k, block=block, slot=slot):
                    load(k, block, slot).start()

    hidden.wait()
    for k in range(4):
        for block in range(m):
            load(k, block, 0).wait()
        held[k] = jnp.dot(mine[...], wide[k], preferred_element_type=F32).astype(BF)
        store(k).start()
    for k in range(4):
        store(k).wait()


def partials(hidden, blocks, slot_of, start, rows):
    full = hidden.shape[1]
    m = len(blocks)
    flat = [w for four in blocks for w in four]
    anywhere = pl.BlockSpec(memory_space=pl.ANY)
    return pl.pallas_call(
        functools.partial(partial_kernel, m, start),
        out_shape=[pltpu.HBM((rows, m * W), BF)] * 4,
        grid_spec=pltpu.PrefetchScalarGridSpec(
            num_scalar_prefetch=1,
            grid=(1,),
            in_specs=[anywhere] * (1 + 4 * m),
            out_specs=[anywhere] * 4,
            scratch_shapes=[
                pltpu.VMEM((rows, full), BF),
                pltpu.VMEM((4, full, m * W), BF),
                pltpu.VMEM((4, rows, m * W), BF),
                pltpu.SemaphoreType.DMA,
                pltpu.SemaphoreType.DMA((4, m)),
                pltpu.SemaphoreType.DMA((4,)),
            ],
        ),
        compiler_params=params(16),
        cost_estimate=COST,
        name="partials",
    )(slot_of, in_hbm(hidden), *flat)


def regroup_kernel(offsets, place, *refs):
    outs = refs[4 * len(offsets) :]
    for s, offs in enumerate(offsets):
        four = refs[4 * s : 4 * s + 4]
        total = four[0][...].astype(F32)
        for ref in four[1:]:
            total += ref[...].astype(F32)
        total = total.astype(BF)
        for block, off in enumerate(offs):
            for which in range(4):

                @pl.when(place[off] == which)
                def _(total=total, block=block, which=which):
                    outs[which][...] = total[:, block * W : (block + 1) * W]


def regroup(groups, place, start, rows):
    tile = rows // 2
    specs, arrays = [], []
    for four, offs in groups:
        first = start // tile if four[0].shape[0] > rows else 0
        spec = pl.BlockSpec((tile, len(offs) * W), lambda i, s, first=first: (first + i, 0))
        specs += [spec] * 4
        arrays += four
    return pl.pallas_call(
        functools.partial(regroup_kernel, [offs for _, offs in groups]),
        out_shape=[pltpu.HBM((rows, W), BF)] * 4,
        grid_spec=pltpu.PrefetchScalarGridSpec(
            num_scalar_prefetch=1,
            grid=(2,),
            in_specs=specs,
            out_specs=[pl.BlockSpec((tile, W), lambda i, s: (i, 0))] * 4,
        ),
        compiler_params=params(16),
        cost_estimate=COST,
        name="regroup",
    )(place, *arrays)


def spread(parts, axis):
    got = [parts[3]] + [shift(parts[k - 1], axis, k) for k in (1, 3, 2)]
    return [in_hbm(part) for part in got] if axis == "x" else got


def finish_kernel(*refs):
    i = pl.program_id(0)
    out = refs[8]
    for which in range(2):

        @pl.when(i == which)
        def _(which=which):
            four = refs[4 * which : 4 * which + 4]
            total = four[0][...].astype(F32)
            for ref in four[1:]:
                total += ref[...].astype(F32)
            out[...] = total.astype(BF)


def finish(first, second):
    rows = first[0].shape[0]
    spec = pl.BlockSpec((rows, W), lambda i: (0, 0))
    return pl.pallas_call(
        finish_kernel,
        out_shape=jax.ShapeDtypeStruct((2 * rows, W), BF),
        grid=(2,),
        in_specs=[spec] * 8,
        out_specs=pl.BlockSpec((rows, W), lambda i: (i, 0)),
        compiler_params=params(12),
        cost_estimate=LIGHT,
        name="finish",
    )(*first, *second)


def low_kernel(parts, out):
    total = parts[0].astype(F32)
    for s in range(1, 4):
        total += parts[s].astype(F32)
    out[...] = total.astype(BF)


def low_sum(parts):
    return pl.pallas_call(
        low_kernel,
        out_shape=jax.ShapeDtypeStruct(parts.shape[1:], BF),
        in_specs=[pl.BlockSpec(memory_space=pltpu.VMEM)],
        out_specs=pl.BlockSpec(memory_space=pltpu.VMEM),
        compiler_params=params(8),
        cost_estimate=COST,
        name="low_sum",
    )(parts)


def grad_kernel(low_ref, cot_ref, out, low):
    @pl.when(pl.program_id(0) == 0)
    def _():
        low_kernel(low_ref, low)

    for block in range(4):
        out[block] = jnp.dot(
            low[...], cot_ref[:, block * W : (block + 1) * W], preferred_element_type=F32
        )


def grad_partial(low_parts, cotangent):
    tokens, features = cotangent.shape
    ranks = low_parts.shape[1]
    return pl.pallas_call(
        grad_kernel,
        out_shape=pltpu.HBM((features // W, ranks, W), F32),
        grid=(features // (4 * W),),
        in_specs=[
            pl.BlockSpec(low_parts.shape, lambda i: (0, 0, 0)),
            pl.BlockSpec((tokens, 4 * W), lambda i: (0, i)),
        ],
        out_specs=pl.BlockSpec((4, ranks, W), lambda i: (i, 0, 0)),
        scratch_shapes=[pltpu.VMEM((ranks, tokens), BF)],
        compiler_params=params(8),
        cost_estimate=COST,
        name="grad_partial",
    )(low_parts, in_hbm(cotangent))


def moments_kernel(grads, first, second, new_first, new_second, normed):
    grad = grads[0]
    for s in range(1, 16):
        grad = grad + grads[s]
    one = 0.9 * first[...] + 0.1 * grad
    two = 0.999 * second[...] + 0.001 * grad * grad
    new_first[...] = one
    new_second[...] = two
    first_fix = 1.0 - 0.9**STEP
    second_fix = 1.0 - 0.999**STEP
    step = (one / first_fix / (jnp.sqrt(two / second_fix) + 1e-08)).astype(BF)
    for s in range(16):
        normed[s] = step


def moments(grads, first, second):
    full = pl.BlockSpec(memory_space=pltpu.VMEM)
    return pl.pallas_call(
        moments_kernel,
        out_shape=[jax.ShapeDtypeStruct(first.shape, F32)] * 2
        + [jax.ShapeDtypeStruct((16, *first.shape), BF)],
        in_specs=[full] * 3,
        out_specs=[full] * 3,
        compiler_params=params(8),
        cost_estimate=LIGHT,
        name="moments",
    )(grads, first, second)


def act_kernel(order, cot_ref, *refs):
    w_refs, out_ref = refs[:16], refs[16]
    cots, wide, total, cot_sems, w_sems = refs[17:]
    span = 4 * W

    def cot_part(i):
        at = pl.multiple_of(order[i] * span, span)
        return pltpu.make_async_copy(cot_ref.at[:, pl.ds(at, span)], cots.at[i], cot_sems.at[i])

    def shard(i, slot):
        at = pl.multiple_of(order[4 + slot] * W, W)
        return pltpu.make_async_copy(
            w_refs[4 * i + slot], wide.at[i, :, pl.ds(at, W)], w_sems.at[i, slot]
        )

    for i in range(4):
        for slot in range(4):
            shard(i, slot).start()
        cot_part(i).start()
    for i in range(4):
        for slot in range(4):
            shard(i, slot).wait()
        cot_part(i).wait()
        product = lax.dot_general(
            cots[i], wide[i], (((1,), (1,)), ((), ())), preferred_element_type=F32
        )
        if i == 0:
            total[...] = product
        elif i < 3:
            total[...] += product
        else:
            out_ref[...] = (total[...] + product).astype(BF)


def act(cotangent, blocks, order):
    tokens, features = cotangent.shape
    flat = [w for four in blocks for w in four]
    full = flat[0].shape[0]
    anywhere = pl.BlockSpec(memory_space=pl.ANY)
    return pl.pallas_call(
        act_kernel,
        out_shape=jax.ShapeDtypeStruct((tokens, full), BF),
        grid_spec=pltpu.PrefetchScalarGridSpec(
            num_scalar_prefetch=1,
            grid=(1,),
            in_specs=[anywhere] * 17,
            out_specs=pl.BlockSpec((tokens, full), lambda i, s: (0, 0)),
            scratch_shapes=[
                pltpu.VMEM((4, tokens, 4 * W), BF),
                pltpu.VMEM((4, full, 4 * W), BF),
                pltpu.VMEM((tokens, full), F32),
                pltpu.SemaphoreType.DMA((4,)),
                pltpu.SemaphoreType.DMA((4, 4)),
            ],
        ),
        compiler_params=params(30),
        cost_estimate=COST,
        name="act_grad",
    )(order, in_hbm(cotangent), *flat)


def on_device(hidden, cotangent, weight, basis, first_moment, second_moment):
    zh, x, y, zl, c = (lax.axis_index(a) for a in AXES)
    tokens = hidden.shape[0]
    half = tokens // 2

    low_part = lax.dot_general(
        basis, hidden, (((0,), (1,)), ((), ())), preferred_element_type=F32
    ).astype(BF)
    low_part = low_part.reshape(4, 4, 32, tokens).transpose(1, 0, 2, 3)

    side = shift(weight, "zl", 1)
    next0, prev0 = shift(weight, "y", -1), shift(weight, "y", 1)
    low_x = swap(after(low_part, weight), "x")
    side = after(side, low_part, next0, prev0)
    next1, prev1 = shift(side, "y", -1), shift(side, "y", 1)

    def both_cores(own, other):
        return own, shift(own, "c", 1), other, shift(other, "c", 1)

    dest = [2 * (zl ^ (s // 2)) + (c ^ (s % 2)) for s in range(4)]
    goals = [(x + k) % 4 for k in (1, 2, 3, 0)]
    slot_of = jnp.stack([2 * ((g // 2) ^ zl) + ((g % 2) ^ c) for g in goals]).astype(jnp.int32)
    place = jnp.stack([(y + k - zh + 3) % 4 for k in range(4)]).astype(jnp.int32)

    slots = {0: both_cores(weight, side)}
    next0c, prev0c = shift(after(next0, low_part), "c", 1), shift(after(prev0, low_part), "c", 1)
    part0 = partials(after(hidden, next0c, prev0c, low_x), [slots[0]], slot_of, 0, tokens)
    sum0 = spread(part0, "x")
    next1c, prev1c = shift(after(next1, *part0), "c", 1), shift(after(prev1, *part0), "c", 1)
    slots[1] = next0, next0c, next1, next1c
    slots[3] = prev0, prev0c, prev1, prev1c
    far0 = shift(after(next0, next1c, prev1c, *part0), "y", -1)
    far1 = shift(after(prev1, next1c, prev1c, *part0), "y", 1)
    near = [[in_hbm(w) for w in slots[off]] for off in (1, 3)]
    part1 = partials(after(hidden, *part0), near, slot_of, 0, half)
    low_z = swap(low_sum(after(low_x, *part1)), "zh")
    slots[2] = both_cores(after(far0, *sum0[1:]), after(far1, *sum0[1:]))
    kept = {0: slots[0], 1: near[0], 3: near[1], 2: [in_hbm(w) for w in slots[2]]}
    kept[0] = [in_hbm(w) for w in kept[0]]
    sum1 = spread(part1, "x")
    part_far = partials(after(hidden, *part1), [kept[2]], slot_of, 0, half)
    sum_far = spread(part_far, "x")

    others = (1, 3, 2)
    part2 = partials(
        after(hidden, low_z, *sum1[1:], *part_far), [kept[off] for off in others], slot_of, half, half
    )
    sum2 = spread(part2, "x")
    zpart1 = regroup(
        [(sum0, (0,)), (sum1, (1, 3)), (sum_far, (2,))], after(place, *part2), 0, half
    )
    got1 = spread(zpart1, "zh")
    grad_all = swap(grad_partial(after(low_z, *part2), cotangent), FSDP)

    new_first, new_second, normed = moments(after(grad_all, *zpart1), first_moment, second_moment)
    normed_all = swap(normed, DP)

    order = jnp.stack([(y + off) % 4 for off in kept] + dest).astype(jnp.int32)
    zpart2 = regroup([(sum0, (0,)), (sum2, others)], after(place, *zpart1), half, half)
    got2 = spread(zpart2, "zh")
    act_grad = act(after(cotangent, *zpart2), list(kept.values()), order)
    normed_all = after(normed_all, *zpart2).reshape(-1, W)
    update = jnp.dot(basis, normed_all, preferred_element_type=F32).astype(BF)
    output = finish(got1, got2)
    return output, act_grad, new_first, new_second, update


def solution(mesh):
    fine = Mesh(mesh.devices.reshape(tuple(SIZE[a] for a in AXES)), AXES)
    in_specs = (
        P(FSDP, DP),
        P(FSDP, None),
        P(DP, FSDP),
        P(DP, None),
        P(DP, FSDP),
        P(DP, FSDP),
    )
    out_specs = (P(FSDP, DP), P(FSDP, DP), P(DP, FSDP), P(DP, FSDP), P(DP, FSDP))
    return jax.shard_map(
        on_device, mesh=fine, in_specs=in_specs, out_specs=out_specs, check_vma=False
    )
```

```python
import functools

import jax
import jax.numpy as jnp
from jax import lax
from jax.experimental import pallas as pl
from jax.experimental.pallas import tpu as pltpu
from jax.sharding import Mesh
from jax.sharding import PartitionSpec as P

STEP = 20
BF = jnp.bfloat16
F32 = jnp.float32
AXES = ("zh", "x", "y", "zl", "c")
SIZE = dict(zh=4, x=4, y=4, zl=2, c=2)
FSDP = ("y", "zl", "c")
DP = ("zh", "x")
W = 256
MIB = 1024 * 1024
LIGHT = pl.CostEstimate(flops=1 << 20, bytes_accessed=1 << 16, transcendentals=0)
COST = pl.CostEstimate(flops=1 << 33, bytes_accessed=1 << 25, transcendentals=0)


def shift(array, axis, by):
    n = SIZE[axis]
    return lax.ppermute(array, axis, [(i, (i + by) % n) for i in range(n)])


def swap(array, axes):
    return lax.all_to_all(array, axes, 0, 0, tiled=True)


def after(value, *others):
    return lax.optimization_barrier((value, *others))[0]


def in_hbm(value):
    return pltpu.with_memory_space_constraint(value, pltpu.HBM)


def params(limit):
    return pltpu.CompilerParams(vmem_limit_bytes=limit * MIB)


def partial_kernel(m, start, slot_of, h_ref, *refs):
    w_refs, outs = refs[: 4 * m], refs[4 * m : 4 * m + 4]
    mine, wide, held, h_sem, w_sems, out_sems = refs[4 * m + 4 :]

    def load(k, block, slot):
        return pltpu.make_async_copy(
            w_refs[4 * block + slot], wide.at[k, :, pl.ds(block * W, W)], w_sems.at[k, block]
        )

    def store(k):
        return pltpu.make_async_copy(held.at[k], outs[k], out_sems.at[k])

    hidden = pltpu.make_async_copy(h_ref.at[pl.ds(start, mine.shape[0])], mine, h_sem)
    hidden.start()
    for k in range(4):
        for block in range(m):
            for slot in range(4):

                @pl.when(slot_of[k] == slot)
                def _(k=k, block=block, slot=slot):
                    load(k, block, slot).start()

    hidden.wait()
    for k in range(4):
        for block in range(m):
            load(k, block, 0).wait()
        held[k] = jnp.dot(mine[...], wide[k], preferred_element_type=F32).astype(BF)
        store(k).start()
    for k in range(4):
        store(k).wait()


def partials(hidden, blocks, slot_of, start, rows):
    full = hidden.shape[1]
    m = len(blocks)
    flat = [w for four in blocks for w in four]
    anywhere = pl.BlockSpec(memory_space=pl.ANY)
    return pl.pallas_call(
        functools.partial(partial_kernel, m, start),
        out_shape=[pltpu.HBM((rows, m * W), BF)] * 4,
        grid_spec=pltpu.PrefetchScalarGridSpec(
            num_scalar_prefetch=1,
            grid=(1,),
            in_specs=[anywhere] * (1 + 4 * m),
            out_specs=[anywhere] * 4,
            scratch_shapes=[
                pltpu.VMEM((rows, full), BF),
                pltpu.VMEM((4, full, m * W), BF),
                pltpu.VMEM((4, rows, m * W), BF),
                pltpu.SemaphoreType.DMA,
                pltpu.SemaphoreType.DMA((4, m)),
                pltpu.SemaphoreType.DMA((4,)),
            ],
        ),
        compiler_params=params(20),
        cost_estimate=COST,
        name="partials",
    )(slot_of, in_hbm(hidden), *flat)


def regroup_kernel(offsets, place, *refs):
    outs = refs[4 * len(offsets) :]
    i = pl.program_id(0)

    def add(group, offs):
        four = refs[4 * group : 4 * group + 4]
        total = four[0][...].astype(F32)
        for ref in four[1:]:
            total += ref[...].astype(F32)
        total = total.astype(BF)
        for block, off in enumerate(offs):
            for which in range(4):

                @pl.when(place[off] == which)
                def _(total=total, block=block, which=which):
                    outs[which][...] = total[:, block * W : (block + 1) * W]

    for group, offs in enumerate(offsets[:-2]):
        add(group, offs)
    pl.when(i < 2)(lambda: add(len(offsets) - 2, offsets[-2]))
    pl.when(i >= 2)(lambda: add(len(offsets) - 1, offsets[-1]))


def regroup(groups, place):
    rows = groups[0][0][0].shape[0]
    tile = rows // 4
    specs, arrays = [], []
    row_of = [lambda i: i] * (len(groups) - 2) + [lambda i: jnp.minimum(i, 1), lambda i: jnp.maximum(i - 2, 0)]
    for (four, offs), row in zip(groups, row_of):
        specs += [pl.BlockSpec((tile, len(offs) * W), lambda i, s, row=row: (row(i), 0))] * 4
        arrays += four
    return pl.pallas_call(
        functools.partial(regroup_kernel, [offs for _, offs in groups]),
        out_shape=[pltpu.HBM((rows, W), BF)] * 4,
        grid_spec=pltpu.PrefetchScalarGridSpec(
            num_scalar_prefetch=1,
            grid=(rows // tile,),
            in_specs=specs,
            out_specs=[pl.BlockSpec((tile, W), lambda i, s: (i, 0))] * 4,
        ),
        compiler_params=params(16),
        cost_estimate=COST,
        name="regroup",
    )(place, *arrays)


def spread(parts, axis):
    got = [parts[3]] + [shift(parts[k - 1], axis, k) for k in (1, 3, 2)]
    return [in_hbm(part) for part in got] if axis == "x" else got


def finish_kernel(a, b, c, d, out):
    total = a[...].astype(F32) + b[...].astype(F32) + c[...].astype(F32) + d[...].astype(F32)
    out[...] = total.astype(BF)


def finish(parts):
    rows = parts[0].shape[0]
    tile = rows // 2
    spec = pl.BlockSpec((tile, W), lambda i: (i, 0))
    return pl.pallas_call(
        finish_kernel,
        out_shape=jax.ShapeDtypeStruct((rows, W), BF),
        grid=(2,),
        in_specs=[spec] * 4,
        out_specs=spec,
        compiler_params=params(12),
        cost_estimate=LIGHT,
        name="finish",
    )(*parts)


def low_kernel(parts, out):
    total = parts[0].astype(F32)
    for s in range(1, 4):
        total += parts[s].astype(F32)
    out[...] = total.astype(BF)


def low_sum(parts):
    return pl.pallas_call(
        low_kernel,
        out_shape=jax.ShapeDtypeStruct(parts.shape[1:], BF),
        in_specs=[pl.BlockSpec(memory_space=pltpu.VMEM)],
        out_specs=pl.BlockSpec(memory_space=pltpu.VMEM),
        compiler_params=params(8),
        cost_estimate=COST,
        name="low_sum",
    )(parts)


def grad_kernel(low_ref, cot_ref, out, low):
    @pl.when(pl.program_id(0) == 0)
    def _():
        low_kernel(low_ref, low)

    for block in range(4):
        out[block] = jnp.dot(
            low[...], cot_ref[:, block * W : (block + 1) * W], preferred_element_type=F32
        )


def grad_partial(low_parts, cotangent):
    tokens, features = cotangent.shape
    ranks = low_parts.shape[1]
    return pl.pallas_call(
        grad_kernel,
        out_shape=pltpu.HBM((features // W, ranks, W), F32),
        grid=(features // (4 * W),),
        in_specs=[
            pl.BlockSpec(low_parts.shape, lambda i: (0, 0, 0)),
            pl.BlockSpec((tokens, 4 * W), lambda i: (0, i)),
        ],
        out_specs=pl.BlockSpec((4, ranks, W), lambda i: (i, 0, 0)),
        scratch_shapes=[pltpu.VMEM((ranks, tokens), BF)],
        compiler_params=params(8),
        cost_estimate=COST,
        name="grad_partial",
    )(low_parts, in_hbm(cotangent))


def moments_kernel(grads, first, second, new_first, new_second, normed):
    grad = grads[0]
    for s in range(1, 16):
        grad = grad + grads[s]
    one = 0.9 * first[...] + 0.1 * grad
    two = 0.999 * second[...] + 0.001 * grad * grad
    new_first[...] = one
    new_second[...] = two
    first_fix = 1.0 - 0.9**STEP
    second_fix = 1.0 - 0.999**STEP
    step = (one / first_fix / (jnp.sqrt(two / second_fix) + 1e-08)).astype(BF)
    for s in range(16):
        normed[s] = step


def moments(grads, first, second):
    full = pl.BlockSpec(memory_space=pltpu.VMEM)
    return pl.pallas_call(
        moments_kernel,
        out_shape=[jax.ShapeDtypeStruct(first.shape, F32)] * 2
        + [jax.ShapeDtypeStruct((16, *first.shape), BF)],
        in_specs=[full] * 3,
        out_specs=[full] * 3,
        compiler_params=params(8),
        cost_estimate=LIGHT,
        name="moments",
    )(grads, first, second)


def act_kernel(order, cot_ref, *refs):
    w_refs, out_ref = refs[:16], refs[16]
    cots, wide, total, cot_sems, w_sems = refs[17:]
    span = 4 * W

    def cot_part(i):
        at = pl.multiple_of(order[i] * span, span)
        return pltpu.make_async_copy(cot_ref.at[:, pl.ds(at, span)], cots.at[i], cot_sems.at[i])

    def shard(i, slot):
        at = pl.multiple_of(order[4 + slot] * W, W)
        return pltpu.make_async_copy(
            w_refs[4 * i + slot], wide.at[i, :, pl.ds(at, W)], w_sems.at[i, slot]
        )

    for i in range(4):
        for slot in range(4):
            shard(i, slot).start()
        cot_part(i).start()
    for i in range(4):
        for slot in range(4):
            shard(i, slot).wait()
        cot_part(i).wait()
        product = lax.dot_general(
            cots[i], wide[i], (((1,), (1,)), ((), ())), preferred_element_type=F32
        )
        if i == 0:
            total[...] = product
        elif i < 3:
            total[...] += product
        else:
            out_ref[...] = (total[...] + product).astype(BF)


def act(cotangent, blocks, order):
    tokens, features = cotangent.shape
    flat = [w for four in blocks for w in four]
    full = flat[0].shape[0]
    anywhere = pl.BlockSpec(memory_space=pl.ANY)
    return pl.pallas_call(
        act_kernel,
        out_shape=jax.ShapeDtypeStruct((tokens, full), BF),
        grid_spec=pltpu.PrefetchScalarGridSpec(
            num_scalar_prefetch=1,
            grid=(1,),
            in_specs=[anywhere] * 17,
            out_specs=pl.BlockSpec((tokens, full), lambda i, s: (0, 0)),
            scratch_shapes=[
                pltpu.VMEM((4, tokens, 4 * W), BF),
                pltpu.VMEM((4, full, 4 * W), BF),
                pltpu.VMEM((tokens, full), F32),
                pltpu.SemaphoreType.DMA((4,)),
                pltpu.SemaphoreType.DMA((4, 4)),
            ],
        ),
        compiler_params=params(30),
        cost_estimate=COST,
        name="act_grad",
    )(order, in_hbm(cotangent), *flat)


def on_device(hidden, cotangent, weight, basis, first_moment, second_moment):
    zh, x, y, zl, c = (lax.axis_index(a) for a in AXES)
    tokens = hidden.shape[0]
    half = tokens // 2

    low_part = lax.dot_general(
        basis, hidden, (((0,), (1,)), ((), ())), preferred_element_type=F32
    ).astype(BF)
    low_part = low_part.reshape(4, 4, 32, tokens).transpose(1, 0, 2, 3)

    side = shift(weight, "zl", 1)
    next0, prev0 = shift(weight, "y", -1), shift(weight, "y", 1)
    low_x = swap(after(low_part, weight), "x")
    side = after(side, low_part, next0, prev0)
    next1, prev1 = shift(side, "y", -1), shift(side, "y", 1)

    def both_cores(own, other):
        return own, shift(own, "c", 1), other, shift(other, "c", 1)

    dest = [2 * (zl ^ (s // 2)) + (c ^ (s % 2)) for s in range(4)]
    goals = [(x + k) % 4 for k in (1, 2, 3, 0)]
    slot_of = jnp.stack([2 * ((g // 2) ^ zl) + ((g % 2) ^ c) for g in goals]).astype(jnp.int32)
    place = jnp.stack([(y + k - zh + 3) % 4 for k in range(4)]).astype(jnp.int32)

    slots = {0: both_cores(weight, side)}
    next0c, prev0c = shift(after(next0, low_part), "c", 1), shift(after(prev0, low_part), "c", 1)
    part0 = partials(after(hidden, next0c, prev0c, low_x), [slots[0]], slot_of, 0, tokens)
    sum0 = spread(part0, "x")
    next1c, prev1c = shift(after(next1, *part0), "c", 1), shift(after(prev1, *part0), "c", 1)
    slots[1] = next0, next0c, next1, next1c
    slots[3] = prev0, prev0c, prev1, prev1c
    far0 = shift(after(next0, next1c, prev1c, *part0), "y", -1)
    far1 = shift(after(prev1, next1c, prev1c, *part0), "y", 1)
    near = [slots[1], slots[3]]
    part1 = partials(after(hidden, *part0), near, slot_of, 0, tokens)
    sum1 = spread(part1, "x")
    slots[2] = both_cores(after(far0, *sum0[1:]), after(far1, *sum0[1:]))
    low_z = swap(low_sum(after(low_x, *part1)), "zh")
    part2 = partials(after(hidden, *part1), [slots[2]], slot_of, 0, half)
    sum2 = spread(part2, "x")
    part3 = partials(after(hidden, *sum1[1:], *part2), [slots[2]], slot_of, half, half)
    sum3 = spread(part3, "x")

    grad_all = swap(grad_partial(after(low_z, *part2), cotangent), FSDP)
    new_first, new_second, normed = moments(grad_all, first_moment, second_moment)
    normed_all = swap(normed, DP)

    order = jnp.stack([(y + off) % 4 for off in slots] + dest).astype(jnp.int32)
    zparts = regroup([(sum0, (0,)), (sum1, (1, 3)), (sum2, (2,)), (sum3, (2,))], place)
    act_grad = act(after(cotangent, *zparts), [[in_hbm(w) for w in four] for four in slots.values()], order)
    normed_all = after(normed_all, *zparts).reshape(-1, W)
    update = jnp.dot(basis, normed_all, preferred_element_type=F32).astype(BF)
    output = finish(spread(zparts, "zh"))
    return output, act_grad, new_first, new_second, update


def solution(mesh):
    fine = Mesh(mesh.devices.reshape(tuple(SIZE[a] for a in AXES)), AXES)
    in_specs = (
        P(FSDP, DP),
        P(FSDP, None),
        P(DP, FSDP),
        P(DP, None),
        P(DP, FSDP),
        P(DP, FSDP),
    )
    out_specs = (P(FSDP, DP), P(FSDP, DP), P(DP, FSDP), P(DP, FSDP), P(DP, FSDP))
    return jax.shard_map(
        on_device, mesh=fine, in_specs=in_specs, out_specs=out_specs, check_vma=False
    )
```

```python
import functools

import jax
import jax.numpy as jnp
from jax import lax
from jax.experimental import pallas as pl
from jax.experimental.pallas import tpu as pltpu
from jax.sharding import Mesh
from jax.sharding import PartitionSpec as P

STEP = 20
BF = jnp.bfloat16
F32 = jnp.float32
AXES = ("zh", "x", "y", "zl", "c")
SIZE = dict(zh=4, x=4, y=4, zl=2, c=2)
FSDP = ("y", "zl", "c")
DP = ("zh", "x")
W = 256
MIB = 1024 * 1024
LIGHT = pl.CostEstimate(flops=1 << 20, bytes_accessed=1 << 16, transcendentals=0)
COST = pl.CostEstimate(flops=1 << 33, bytes_accessed=1 << 25, transcendentals=0)


def shift(array, axis, by):
    n = SIZE[axis]
    return lax.ppermute(array, axis, [(i, (i + by) % n) for i in range(n)])


def swap(array, axes):
    return lax.all_to_all(array, axes, 0, 0, tiled=True)


def after(value, *others):
    return lax.optimization_barrier((value, *others))[0]


def in_hbm(value):
    return pltpu.with_memory_space_constraint(value, pltpu.HBM)


def params(limit):
    return pltpu.CompilerParams(vmem_limit_bytes=limit * MIB)


def partial_kernel(m, start, slot_of, h_ref, *refs):
    w_refs, outs = refs[: 4 * m], refs[4 * m : 4 * m + 4]
    mine, wide, held, h_sem, w_sems, out_sems = refs[4 * m + 4 :]

    def load(k, block, slot):
        return pltpu.make_async_copy(
            w_refs[4 * block + slot], wide.at[k, :, pl.ds(block * W, W)], w_sems.at[k, block]
        )

    def store(k):
        return pltpu.make_async_copy(held.at[k], outs[k], out_sems.at[k])

    hidden = pltpu.make_async_copy(h_ref.at[pl.ds(start, mine.shape[0])], mine, h_sem)
    hidden.start()
    for k in range(4):
        for block in range(m):
            for slot in range(4):

                @pl.when(slot_of[k] == slot)
                def _(k=k, block=block, slot=slot):
                    load(k, block, slot).start()

    hidden.wait()
    for k in range(4):
        for block in range(m):
            load(k, block, 0).wait()
        held[k] = jnp.dot(mine[...], wide[k], preferred_element_type=F32).astype(BF)
        store(k).start()
    for k in range(4):
        store(k).wait()


def partials(hidden, blocks, slot_of, start, rows):
    full = hidden.shape[1]
    m = len(blocks)
    flat = [w for four in blocks for w in four]
    anywhere = pl.BlockSpec(memory_space=pl.ANY)
    return pl.pallas_call(
        functools.partial(partial_kernel, m, start),
        out_shape=[pltpu.HBM((rows, m * W), BF)] * 4,
        grid_spec=pltpu.PrefetchScalarGridSpec(
            num_scalar_prefetch=1,
            grid=(1,),
            in_specs=[anywhere] * (1 + 4 * m),
            out_specs=[anywhere] * 4,
            scratch_shapes=[
                pltpu.VMEM((rows, full), BF),
                pltpu.VMEM((4, full, m * W), BF),
                pltpu.VMEM((4, rows, m * W), BF),
                pltpu.SemaphoreType.DMA,
                pltpu.SemaphoreType.DMA((4, m)),
                pltpu.SemaphoreType.DMA((4,)),
            ],
        ),
        compiler_params=params(20),
        cost_estimate=COST,
        name="partials",
    )(slot_of, in_hbm(hidden), *flat)


def regroup_kernel(offsets, place, *refs):
    outs = refs[4 * len(offsets) :]
    i = pl.program_id(0)

    def add(group, offs):
        four = refs[4 * group : 4 * group + 4]
        total = four[0][...].astype(F32)
        for ref in four[1:]:
            total += ref[...].astype(F32)
        total = total.astype(BF)
        for block, off in enumerate(offs):
            for which in range(4):

                @pl.when(place[off] == which)
                def _(total=total, block=block, which=which):
                    outs[which][...] = total[:, block * W : (block + 1) * W]

    for group, offs in enumerate(offsets[:-2]):
        add(group, offs)
    pl.when(i < 2)(lambda: add(len(offsets) - 2, offsets[-2]))
    pl.when(i >= 2)(lambda: add(len(offsets) - 1, offsets[-1]))


def regroup(groups, place):
    rows = groups[0][0][0].shape[0]
    tile = rows // 4
    specs, arrays = [], []
    row_of = [lambda i: i] * (len(groups) - 2) + [lambda i: jnp.minimum(i, 1), lambda i: jnp.maximum(i - 2, 0)]
    for (four, offs), row in zip(groups, row_of):
        specs += [pl.BlockSpec((tile, len(offs) * W), lambda i, s, row=row: (row(i), 0))] * 4
        arrays += four
    return pl.pallas_call(
        functools.partial(regroup_kernel, [offs for _, offs in groups]),
        out_shape=[pltpu.HBM((rows, W), BF)] * 4,
        grid_spec=pltpu.PrefetchScalarGridSpec(
            num_scalar_prefetch=1,
            grid=(rows // tile,),
            in_specs=specs,
            out_specs=[pl.BlockSpec((tile, W), lambda i, s: (i, 0))] * 4,
        ),
        compiler_params=params(16),
        cost_estimate=COST,
        name="regroup",
    )(place, *arrays)


def spread(parts, axis):
    got = [parts[3]] + [shift(parts[k - 1], axis, k) for k in (1, 3, 2)]
    return [in_hbm(part) for part in got] if axis == "x" else got


def finish_kernel(a, b, c, d, out):
    total = a[...].astype(F32) + b[...].astype(F32) + c[...].astype(F32) + d[...].astype(F32)
    out[...] = total.astype(BF)


def finish(parts):
    rows = parts[0].shape[0]
    tile = rows // 2
    spec = pl.BlockSpec((tile, W), lambda i: (i, 0))
    return pl.pallas_call(
        finish_kernel,
        out_shape=jax.ShapeDtypeStruct((rows, W), BF),
        grid=(2,),
        in_specs=[spec] * 4,
        out_specs=spec,
        compiler_params=params(12),
        cost_estimate=LIGHT,
        name="finish",
    )(*parts)


def low_kernel(parts, out):
    total = parts[0].astype(F32)
    for s in range(1, 4):
        total += parts[s].astype(F32)
    out[...] = total.astype(BF)


def low_sum(parts):
    return pl.pallas_call(
        low_kernel,
        out_shape=jax.ShapeDtypeStruct(parts.shape[1:], BF),
        in_specs=[pl.BlockSpec(memory_space=pltpu.VMEM)],
        out_specs=pl.BlockSpec(memory_space=pltpu.VMEM),
        compiler_params=params(8),
        cost_estimate=COST,
        name="low_sum",
    )(parts)


def grad_kernel(low_ref, cot_ref, out, low):
    @pl.when(pl.program_id(0) == 0)
    def _():
        low_kernel(low_ref, low)

    for block in range(4):
        out[block] = jnp.dot(
            low[...], cot_ref[:, block * W : (block + 1) * W], preferred_element_type=F32
        )


def grad_partial(low_parts, cotangent):
    tokens, features = cotangent.shape
    ranks = low_parts.shape[1]
    return pl.pallas_call(
        grad_kernel,
        out_shape=pltpu.HBM((features // W, ranks, W), F32),
        grid=(features // (4 * W),),
        in_specs=[
            pl.BlockSpec(low_parts.shape, lambda i: (0, 0, 0)),
            pl.BlockSpec((tokens, 4 * W), lambda i: (0, i)),
        ],
        out_specs=pl.BlockSpec((4, ranks, W), lambda i: (i, 0, 0)),
        scratch_shapes=[pltpu.VMEM((ranks, tokens), BF)],
        compiler_params=params(8),
        cost_estimate=COST,
        name="grad_partial",
    )(low_parts, in_hbm(cotangent))


def moments_kernel(grads, first, second, new_first, new_second, normed):
    grad = grads[0]
    for s in range(1, 16):
        grad = grad + grads[s]
    one = 0.9 * first[...] + 0.1 * grad
    two = 0.999 * second[...] + 0.001 * grad * grad
    new_first[...] = one
    new_second[...] = two
    first_fix = 1.0 - 0.9**STEP
    second_fix = 1.0 - 0.999**STEP
    step = (one / first_fix / (jnp.sqrt(two / second_fix) + 1e-08)).astype(BF)
    for s in range(16):
        normed[s] = step


def moments(grads, first, second):
    full = pl.BlockSpec(memory_space=pltpu.VMEM)
    return pl.pallas_call(
        moments_kernel,
        out_shape=[jax.ShapeDtypeStruct(first.shape, F32)] * 2
        + [jax.ShapeDtypeStruct((16, *first.shape), BF)],
        in_specs=[full] * 3,
        out_specs=[full] * 3,
        compiler_params=params(8),
        cost_estimate=LIGHT,
        name="moments",
    )(grads, first, second)


def act_kernel(order, cot_ref, *refs):
    w_refs, out_ref = refs[:16], refs[16]
    cots, wide, total, cot_sems, w_sems = refs[17:]
    span = 4 * W

    def cot_part(i):
        at = pl.multiple_of(order[i] * span, span)
        return pltpu.make_async_copy(cot_ref.at[:, pl.ds(at, span)], cots.at[i], cot_sems.at[i])

    def shard(i, slot):
        at = pl.multiple_of(order[4 + slot] * W, W)
        return pltpu.make_async_copy(
            w_refs[4 * i + slot], wide.at[i, :, pl.ds(at, W)], w_sems.at[i, slot]
        )

    for i in range(4):
        for slot in range(4):
            shard(i, slot).start()
        cot_part(i).start()
    for i in range(4):
        for slot in range(4):
            shard(i, slot).wait()
        cot_part(i).wait()
        product = lax.dot_general(
            cots[i], wide[i], (((1,), (1,)), ((), ())), preferred_element_type=F32
        )
        if i == 0:
            total[...] = product
        elif i < 3:
            total[...] += product
        else:
            out_ref[...] = (total[...] + product).astype(BF)


def act(cotangent, blocks, order):
    tokens, features = cotangent.shape
    flat = [w for four in blocks for w in four]
    full = flat[0].shape[0]
    anywhere = pl.BlockSpec(memory_space=pl.ANY)
    return pl.pallas_call(
        act_kernel,
        out_shape=jax.ShapeDtypeStruct((tokens, full), BF),
        grid_spec=pltpu.PrefetchScalarGridSpec(
            num_scalar_prefetch=1,
            grid=(1,),
            in_specs=[anywhere] * 17,
            out_specs=pl.BlockSpec((tokens, full), lambda i, s: (0, 0)),
            scratch_shapes=[
                pltpu.VMEM((4, tokens, 4 * W), BF),
                pltpu.VMEM((4, full, 4 * W), BF),
                pltpu.VMEM((tokens, full), F32),
                pltpu.SemaphoreType.DMA((4,)),
                pltpu.SemaphoreType.DMA((4, 4)),
            ],
        ),
        compiler_params=params(30),
        cost_estimate=COST,
        name="act_grad",
    )(order, in_hbm(cotangent), *flat)


def on_device(hidden, cotangent, weight, basis, first_moment, second_moment):
    zh, x, y, zl, c = (lax.axis_index(a) for a in AXES)
    tokens = hidden.shape[0]
    half = tokens // 2

    low_part = lax.dot_general(
        basis, hidden, (((0,), (1,)), ((), ())), preferred_element_type=F32
    ).astype(BF)
    low_part = low_part.reshape(4, 4, 32, tokens).transpose(1, 0, 2, 3)

    side = shift(weight, "zl", 1)
    next0, prev0 = shift(weight, "y", -1), shift(weight, "y", 1)
    low_x = swap(after(low_part, weight), "x")
    side = after(side, low_part, next0, prev0)
    next1, prev1 = shift(side, "y", -1), shift(side, "y", 1)

    def both_cores(own, other):
        return own, shift(own, "c", 1), other, shift(other, "c", 1)

    dest = [2 * (zl ^ (s // 2)) + (c ^ (s % 2)) for s in range(4)]
    goals = [(x + k) % 4 for k in (1, 2, 3, 0)]
    slot_of = jnp.stack([2 * ((g // 2) ^ zl) + ((g % 2) ^ c) for g in goals]).astype(jnp.int32)
    place = jnp.stack([(y + k - zh + 3) % 4 for k in range(4)]).astype(jnp.int32)

    slots = {0: both_cores(weight, side)}
    next0c, prev0c = shift(after(next0, low_part), "c", 1), shift(after(prev0, low_part), "c", 1)
    part0 = partials(after(hidden, next0c, prev0c, low_x), [slots[0]], slot_of, 0, tokens)
    sum0 = spread(part0, "x")
    next1c, prev1c = shift(after(next1, *part0), "c", 1), shift(after(prev1, *part0), "c", 1)
    slots[1] = next0, next0c, next1, next1c
    slots[3] = prev0, prev0c, prev1, prev1c
    far0 = shift(after(next0, next1c, prev1c, *part0), "y", -1)
    far1 = shift(after(prev1, next1c, prev1c, *part0), "y", 1)
    near = [slots[1], slots[3]]
    part1 = partials(after(hidden, *part0), near, slot_of, 0, tokens)
    sum1 = spread(part1, "x")
    slots[2] = both_cores(after(far0, *sum0[1:]), after(far1, *sum0[1:]))
    low_z = swap(low_sum(after(low_x, *part1)), "zh")
    part2 = partials(after(hidden, *part1), [slots[2]], slot_of, 0, half)
    sum2 = spread(part2, "x")
    grad_part = grad_partial(after(low_z, *part2), cotangent)
    grad_all = swap(grad_part, FSDP)
    part3 = partials(after(hidden, grad_part, *sum1[1:], *part2), [slots[2]], slot_of, half, half)
    sum3 = spread(part3, "x")

    new_first, new_second, normed = moments(grad_all, first_moment, second_moment)
    normed_all = swap(normed, DP)

    order = jnp.stack([(y + off) % 4 for off in slots] + dest).astype(jnp.int32)
    zparts = regroup([(sum0, (0,)), (sum1, (1, 3)), (sum2, (2,)), (sum3, (2,))], after(place, normed))
    act_grad = act(after(cotangent, *zparts), [[in_hbm(w) for w in four] for four in slots.values()], order)
    normed_all = after(normed_all, *zparts).reshape(-1, W)
    update = jnp.dot(basis, normed_all, preferred_element_type=F32).astype(BF)
    output = finish(spread(zparts, "zh"))
    return output, act_grad, new_first, new_second, update


def solution(mesh):
    fine = Mesh(mesh.devices.reshape(tuple(SIZE[a] for a in AXES)), AXES)
    in_specs = (
        P(FSDP, DP),
        P(FSDP, None),
        P(DP, FSDP),
        P(DP, None),
        P(DP, FSDP),
        P(DP, FSDP),
    )
    out_specs = (P(FSDP, DP), P(FSDP, DP), P(DP, FSDP), P(DP, FSDP), P(DP, FSDP))
    return jax.shard_map(
        on_device, mesh=fine, in_specs=in_specs, out_specs=out_specs, check_vma=False
    )
```

```python
import functools

import jax
import jax.numpy as jnp
from jax import lax
from jax.experimental import pallas as pl
from jax.experimental.pallas import tpu as pltpu
from jax.sharding import Mesh
from jax.sharding import PartitionSpec as P

STEP = 20
BF = jnp.bfloat16
F32 = jnp.float32
AXES = ("zh", "x", "y", "zl", "c")
SIZE = dict(zh=4, x=4, y=4, zl=2, c=2)
FSDP = ("y", "zl", "c")
DP = ("zh", "x")
W = 256
MIB = 1024 * 1024
LIGHT = pl.CostEstimate(flops=1 << 20, bytes_accessed=1 << 16, transcendentals=0)
COST = pl.CostEstimate(flops=1 << 33, bytes_accessed=1 << 25, transcendentals=0)


def shift(array, axis, by):
    n = SIZE[axis]
    return lax.ppermute(array, axis, [(i, (i + by) % n) for i in range(n)])


def swap(array, axes):
    return lax.all_to_all(array, axes, 0, 0, tiled=True)


def after(value, *others):
    return lax.optimization_barrier((value, *others))[0]


def in_hbm(value):
    return pltpu.with_memory_space_constraint(value, pltpu.HBM)


def params(limit):
    return pltpu.CompilerParams(vmem_limit_bytes=limit * MIB)


def partial_kernel(m, start, slot_of, h_ref, *refs):
    w_refs, outs = refs[: 4 * m], refs[4 * m : 4 * m + 4]
    mine, wide, held, h_sem, w_sems, out_sems = refs[4 * m + 4 :]

    def load(k, block, slot):
        return pltpu.make_async_copy(
            w_refs[4 * block + slot], wide.at[k, :, pl.ds(block * W, W)], w_sems.at[k, block]
        )

    def store(k):
        return pltpu.make_async_copy(held.at[k], outs[k], out_sems.at[k])

    hidden = pltpu.make_async_copy(h_ref.at[pl.ds(start, mine.shape[0])], mine, h_sem)
    hidden.start()
    for k in range(4):
        for block in range(m):
            for slot in range(4):

                @pl.when(slot_of[k] == slot)
                def _(k=k, block=block, slot=slot):
                    load(k, block, slot).start()

    hidden.wait()
    for k in range(4):
        for block in range(m):
            load(k, block, 0).wait()
        held[k] = jnp.dot(mine[...], wide[k], preferred_element_type=F32).astype(BF)
        store(k).start()
    for k in range(4):
        store(k).wait()


def partials(hidden, blocks, slot_of, start, rows):
    full = hidden.shape[1]
    m = len(blocks)
    flat = [w for four in blocks for w in four]
    anywhere = pl.BlockSpec(memory_space=pl.ANY)
    return pl.pallas_call(
        functools.partial(partial_kernel, m, start),
        out_shape=[pltpu.HBM((rows, m * W), BF)] * 4,
        grid_spec=pltpu.PrefetchScalarGridSpec(
            num_scalar_prefetch=1,
            grid=(1,),
            in_specs=[anywhere] * (1 + 4 * m),
            out_specs=[anywhere] * 4,
            scratch_shapes=[
                pltpu.VMEM((rows, full), BF),
                pltpu.VMEM((4, full, m * W), BF),
                pltpu.VMEM((4, rows, m * W), BF),
                pltpu.SemaphoreType.DMA,
                pltpu.SemaphoreType.DMA((4, m)),
                pltpu.SemaphoreType.DMA((4,)),
            ],
        ),
        compiler_params=params(20),
        cost_estimate=COST,
        name="partials",
    )(slot_of, in_hbm(hidden), *flat)


def regroup_kernel(offsets, place, *refs):
    outs = refs[4 * len(offsets) :]
    i = pl.program_id(0)

    def add(group, offs):
        four = refs[4 * group : 4 * group + 4]
        total = four[0][...].astype(F32)
        for ref in four[1:]:
            total += ref[...].astype(F32)
        total = total.astype(BF)
        for block, off in enumerate(offs):
            for which in range(4):

                @pl.when(place[off] == which)
                def _(total=total, block=block, which=which):
                    outs[which][...] = total[:, block * W : (block + 1) * W]

    for group, offs in enumerate(offsets[:-2]):
        add(group, offs)
    pl.when(i == 0)(lambda: add(len(offsets) - 2, offsets[-2]))
    pl.when(i == 1)(lambda: add(len(offsets) - 1, offsets[-1]))


def regroup(groups, place):
    rows = groups[0][0][0].shape[0]
    tile = rows // 2
    specs, arrays = [], []
    row_of = [lambda i: i] * (len(groups) - 2) + [lambda i: 0] * 2
    for (four, offs), row in zip(groups, row_of):
        specs += [pl.BlockSpec((tile, len(offs) * W), lambda i, s, row=row: (row(i), 0))] * 4
        arrays += four
    return pl.pallas_call(
        functools.partial(regroup_kernel, [offs for _, offs in groups]),
        out_shape=[pltpu.HBM((rows, W), BF)] * 4,
        grid_spec=pltpu.PrefetchScalarGridSpec(
            num_scalar_prefetch=1,
            grid=(rows // tile,),
            in_specs=specs,
            out_specs=[pl.BlockSpec((tile, W), lambda i, s: (i, 0))] * 4,
        ),
        compiler_params=params(24),
        cost_estimate=COST,
        name="regroup",
    )(place, *arrays)


def spread(parts, axis):
    got = [parts[3]] + [shift(parts[k - 1], axis, k) for k in (1, 3, 2)]
    return [in_hbm(part) for part in got] if axis == "x" else got


def finish_kernel(a, b, c, d, out):
    total = a[...].astype(F32) + b[...].astype(F32) + c[...].astype(F32) + d[...].astype(F32)
    out[...] = total.astype(BF)


def finish(parts):
    rows = parts[0].shape[0]
    tile = rows // 2
    spec = pl.BlockSpec((tile, W), lambda i: (i, 0))
    return pl.pallas_call(
        finish_kernel,
        out_shape=jax.ShapeDtypeStruct((rows, W), BF),
        grid=(2,),
        in_specs=[spec] * 4,
        out_specs=spec,
        compiler_params=params(12),
        cost_estimate=LIGHT,
        name="finish",
    )(*parts)


def grad_kernel(low_ref, cot_ref, out):
    for block in range(4):
        out[block] = jnp.dot(
            low_ref[...], cot_ref[:, block * W : (block + 1) * W], preferred_element_type=F32
        )


def grad_partial(low, cotangent):
    tokens, features = cotangent.shape
    ranks = low.shape[0]
    return pl.pallas_call(
        grad_kernel,
        out_shape=pltpu.HBM((features // W, ranks, W), F32),
        grid=(features // (4 * W),),
        in_specs=[
            pl.BlockSpec((ranks, tokens), lambda i: (0, 0)),
            pl.BlockSpec((tokens, 4 * W), lambda i: (0, i)),
        ],
        out_specs=pl.BlockSpec((4, ranks, W), lambda i: (i, 0, 0)),
        compiler_params=params(8),
        cost_estimate=COST,
        name="grad_partial",
    )(low, in_hbm(cotangent))


def moments_kernel(grads, first, second, new_first, new_second, normed):
    grad = grads[0]
    for s in range(1, 16):
        grad = grad + grads[s]
    one = 0.9 * first[...] + 0.1 * grad
    two = 0.999 * second[...] + 0.001 * grad * grad
    new_first[...] = one
    new_second[...] = two
    first_fix = 1.0 - 0.9**STEP
    second_fix = 1.0 - 0.999**STEP
    step = (one / first_fix / (jnp.sqrt(two / second_fix) + 1e-08)).astype(BF)
    for s in range(16):
        normed[s] = step


def moments(grads, first, second):
    full = pl.BlockSpec(memory_space=pltpu.VMEM)
    return pl.pallas_call(
        moments_kernel,
        out_shape=[jax.ShapeDtypeStruct(first.shape, F32)] * 2
        + [jax.ShapeDtypeStruct((16, *first.shape), BF)],
        in_specs=[full] * 3,
        out_specs=[full] * 3,
        compiler_params=params(8),
        cost_estimate=LIGHT,
        name="moments",
    )(grads, first, second)


def act_kernel(order, cot_ref, *refs):
    w_refs, out_ref = refs[:16], refs[16]
    cots, wide, total, cot_sems, w_sems = refs[17:]
    span = 4 * W

    def cot_part(i):
        at = pl.multiple_of(order[i] * span, span)
        return pltpu.make_async_copy(cot_ref.at[:, pl.ds(at, span)], cots.at[i], cot_sems.at[i])

    def shard(i, slot):
        at = pl.multiple_of(order[4 + slot] * W, W)
        return pltpu.make_async_copy(
            w_refs[4 * i + slot], wide.at[i, :, pl.ds(at, W)], w_sems.at[i, slot]
        )

    for i in range(4):
        for slot in range(4):
            shard(i, slot).start()
        cot_part(i).start()
    for i in range(4):
        for slot in range(4):
            shard(i, slot).wait()
        cot_part(i).wait()
        product = lax.dot_general(
            cots[i], wide[i], (((1,), (1,)), ((), ())), preferred_element_type=F32
        )
        if i == 0:
            total[...] = product
        elif i < 3:
            total[...] += product
        else:
            out_ref[...] = (total[...] + product).astype(BF)


def act(cotangent, blocks, order):
    tokens, features = cotangent.shape
    flat = [w for four in blocks for w in four]
    full = flat[0].shape[0]
    anywhere = pl.BlockSpec(memory_space=pl.ANY)
    return pl.pallas_call(
        act_kernel,
        out_shape=jax.ShapeDtypeStruct((tokens, full), BF),
        grid_spec=pltpu.PrefetchScalarGridSpec(
            num_scalar_prefetch=1,
            grid=(1,),
            in_specs=[anywhere] * 17,
            out_specs=pl.BlockSpec((tokens, full), lambda i, s: (0, 0)),
            scratch_shapes=[
                pltpu.VMEM((4, tokens, 4 * W), BF),
                pltpu.VMEM((4, full, 4 * W), BF),
                pltpu.VMEM((tokens, full), F32),
                pltpu.SemaphoreType.DMA((4,)),
                pltpu.SemaphoreType.DMA((4, 4)),
            ],
        ),
        compiler_params=params(30),
        cost_estimate=COST,
        name="act_grad",
    )(order, in_hbm(cotangent), *flat)


def on_device(hidden, cotangent, weight, basis, first_moment, second_moment):
    zh, x, y, zl, c = (lax.axis_index(a) for a in AXES)
    tokens = hidden.shape[0]
    half = tokens // 2

    low_part = lax.dot_general(
        basis, hidden, (((0,), (1,)), ((), ())), preferred_element_type=F32
    )
    low = lax.psum_scatter(low_part, DP, scatter_dimension=0, tiled=True).astype(BF)

    side = shift(weight, "zl", 1)
    next0, prev0 = shift(weight, "y", -1), shift(weight, "y", 1)
    side = after(side, low_part, next0, prev0)
    next1, prev1 = shift(side, "y", -1), shift(side, "y", 1)

    def both_cores(own, other):
        return own, shift(own, "c", 1), other, shift(other, "c", 1)

    dest = [2 * (zl ^ (s // 2)) + (c ^ (s % 2)) for s in range(4)]
    goals = [(x + k) % 4 for k in (1, 2, 3, 0)]
    slot_of = jnp.stack([2 * ((g // 2) ^ zl) + ((g % 2) ^ c) for g in goals]).astype(jnp.int32)
    place = jnp.stack([(y + k - zh + 3) % 4 for k in range(4)]).astype(jnp.int32)

    slots = {0: both_cores(weight, side)}
    next0c, prev0c = shift(after(next0, low_part), "c", 1), shift(after(prev0, low_part), "c", 1)
    part0 = partials(after(hidden, next0c, prev0c), [slots[0]], slot_of, 0, tokens)
    sum0 = spread(part0, "x")
    next1c, prev1c = shift(after(next1, *part0), "c", 1), shift(after(prev1, *part0), "c", 1)
    slots[1] = next0, next0c, next1, next1c
    slots[3] = prev0, prev0c, prev1, prev1c
    far0 = shift(after(next0, next1c, prev1c, *part0), "y", -1)
    far1 = shift(after(prev1, next1c, prev1c, *part0), "y", 1)
    near = [slots[1], slots[3]]
    part1 = partials(after(hidden, *part0), near, slot_of, 0, tokens)
    sum1 = spread(part1, "x")
    slots[2] = both_cores(after(far0, *sum0[1:], *part1), after(far1, *sum0[1:], *part1))
    part2 = partials(after(hidden, *part1), [slots[2]], slot_of, 0, half)
    sum2 = spread(part2, "x")
    grad_part = grad_partial(after(low, *part2), cotangent)
    grad_all = swap(grad_part, FSDP)
    part3 = partials(after(hidden, grad_part, *sum1[1:], *part2), [slots[2]], slot_of, half, half)
    sum3 = spread(part3, "x")

    new_first, new_second, normed = moments(grad_all, first_moment, second_moment)
    normed_all = swap(normed, DP)

    order = jnp.stack([(y + off) % 4 for off in slots] + dest).astype(jnp.int32)
    zparts = regroup([(sum0, (0,)), (sum1, (1, 3)), (sum2, (2,)), (sum3, (2,))], after(place, normed))
    act_grad = act(after(cotangent, *zparts), [[in_hbm(w) for w in four] for four in slots.values()], order)
    normed_all = after(normed_all, *zparts).reshape(-1, W)
    update = jnp.dot(basis, normed_all, preferred_element_type=F32).astype(BF)
    output = finish(spread(zparts, "zh"))
    return output, act_grad, new_first, new_second, update


def solution(mesh):
    fine = Mesh(mesh.devices.reshape(tuple(SIZE[a] for a in AXES)), AXES)
    in_specs = (
        P(FSDP, DP),
        P(FSDP, None),
        P(DP, FSDP),
        P(DP, None),
        P(DP, FSDP),
        P(DP, FSDP),
    )
    out_specs = (P(FSDP, DP), P(FSDP, DP), P(DP, FSDP), P(DP, FSDP), P(DP, FSDP))
    return jax.shard_map(
        on_device, mesh=fine, in_specs=in_specs, out_specs=out_specs, check_vma=False
    )
```

```python
import functools

import jax
import jax.numpy as jnp
from jax import lax
from jax.experimental import pallas as pl
from jax.experimental.pallas import tpu as pltpu
from jax.sharding import Mesh
from jax.sharding import PartitionSpec as P

STEP = 20
BF = jnp.bfloat16
F32 = jnp.float32
AXES = ("zh", "x", "y", "zl", "c")
SIZE = dict(zh=4, x=4, y=4, zl=2, c=2)
FSDP = ("y", "zl", "c")
DP = ("zh", "x")
W = 256
MIB = 1024 * 1024
LIGHT = pl.CostEstimate(flops=1 << 20, bytes_accessed=1 << 16, transcendentals=0)
COST = pl.CostEstimate(flops=1 << 33, bytes_accessed=1 << 25, transcendentals=0)


def shift(array, axis, by):
    n = SIZE[axis]
    return lax.ppermute(array, axis, [(i, (i + by) % n) for i in range(n)])


def swap(array, axes):
    return lax.all_to_all(array, axes, 0, 0, tiled=True)


def after(value, *others):
    return lax.optimization_barrier((value, *others))[0]


def in_hbm(value):
    return pltpu.with_memory_space_constraint(value, pltpu.HBM)


def params(limit):
    return pltpu.CompilerParams(vmem_limit_bytes=limit * MIB)


def partial_kernel(m, start, slot_of, h_ref, *refs):
    w_refs, outs = refs[: 4 * m], refs[4 * m : 4 * m + 4]
    mine, wide, held, h_sem, w_sems, out_sems = refs[4 * m + 4 :]

    def load(k, block, slot):
        return pltpu.make_async_copy(
            w_refs[4 * block + slot], wide.at[k, :, pl.ds(block * W, W)], w_sems.at[k, block]
        )

    def store(k):
        return pltpu.make_async_copy(held.at[k], outs[k], out_sems.at[k])

    hidden = pltpu.make_async_copy(h_ref.at[pl.ds(start, mine.shape[0])], mine, h_sem)
    hidden.start()
    for k in range(4):
        for block in range(m):
            for slot in range(4):

                @pl.when(slot_of[k] == slot)
                def _(k=k, block=block, slot=slot):
                    load(k, block, slot).start()

    hidden.wait()
    for k in range(4):
        for block in range(m):
            load(k, block, 0).wait()
        held[k] = jnp.dot(mine[...], wide[k], preferred_element_type=F32).astype(BF)
        store(k).start()
    for k in range(4):
        store(k).wait()


def partials(hidden, blocks, slot_of, start, rows):
    full = hidden.shape[1]
    m = len(blocks)
    flat = [w for four in blocks for w in four]
    anywhere = pl.BlockSpec(memory_space=pl.ANY)
    return pl.pallas_call(
        functools.partial(partial_kernel, m, start),
        out_shape=[pltpu.HBM((rows, m * W), BF)] * 4,
        grid_spec=pltpu.PrefetchScalarGridSpec(
            num_scalar_prefetch=1,
            grid=(1,),
            in_specs=[anywhere] * (1 + 4 * m),
            out_specs=[anywhere] * 4,
            scratch_shapes=[
                pltpu.VMEM((rows, full), BF),
                pltpu.VMEM((4, full, m * W), BF),
                pltpu.VMEM((4, rows, m * W), BF),
                pltpu.SemaphoreType.DMA,
                pltpu.SemaphoreType.DMA((4, m)),
                pltpu.SemaphoreType.DMA((4,)),
            ],
        ),
        compiler_params=params(20),
        cost_estimate=COST,
        name="partials",
    )(slot_of, in_hbm(hidden), *flat)


def regroup_kernel(offsets, place, *refs):
    outs = refs[4 * len(offsets) :]
    i = pl.program_id(0)

    def add(group, offs):
        four = refs[4 * group : 4 * group + 4]
        total = four[0][...].astype(F32)
        for ref in four[1:]:
            total += ref[...].astype(F32)
        total = total.astype(BF)
        for block, off in enumerate(offs):
            for which in range(4):

                @pl.when(place[off] == which)
                def _(total=total, block=block, which=which):
                    outs[which][...] = total[:, block * W : (block + 1) * W]

    for group, offs in enumerate(offsets[:-2]):
        add(group, offs)
    pl.when(i < 2)(lambda: add(len(offsets) - 2, offsets[-2]))
    pl.when(i >= 2)(lambda: add(len(offsets) - 1, offsets[-1]))


def regroup(groups, place):
    rows = groups[0][0][0].shape[0]
    tile = rows // 4
    specs, arrays = [], []
    row_of = [lambda i: i] * (len(groups) - 2) + [lambda i: jnp.minimum(i, 1), lambda i: jnp.maximum(i - 2, 0)]
    for (four, offs), row in zip(groups, row_of):
        specs += [pl.BlockSpec((tile, len(offs) * W), lambda i, s, row=row: (row(i), 0))] * 4
        arrays += four
    return pl.pallas_call(
        functools.partial(regroup_kernel, [offs for _, offs in groups]),
        out_shape=[pltpu.HBM((rows, W), BF)] * 4,
        grid_spec=pltpu.PrefetchScalarGridSpec(
            num_scalar_prefetch=1,
            grid=(rows // tile,),
            in_specs=specs,
            out_specs=[pl.BlockSpec((tile, W), lambda i, s: (i, 0))] * 4,
        ),
        compiler_params=params(16),
        cost_estimate=COST,
        name="regroup",
    )(place, *arrays)


def spread(parts, axis):
    got = [parts[3]] + [shift(parts[k - 1], axis, k) for k in (1, 3, 2)]
    return [in_hbm(part) for part in got] if axis == "x" else got


def finish_kernel(a, b, c, d, out):
    total = a[...].astype(F32) + b[...].astype(F32) + c[...].astype(F32) + d[...].astype(F32)
    out[...] = total.astype(BF)


def finish(parts):
    rows = parts[0].shape[0]
    tile = rows // 2
    spec = pl.BlockSpec((tile, W), lambda i: (i, 0))
    return pl.pallas_call(
        finish_kernel,
        out_shape=jax.ShapeDtypeStruct((rows, W), BF),
        grid=(2,),
        in_specs=[spec] * 4,
        out_specs=spec,
        compiler_params=params(12),
        cost_estimate=LIGHT,
        name="finish",
    )(*parts)


def low_kernel(parts, out):
    total = parts[0].astype(F32)
    for s in range(1, 4):
        total += parts[s].astype(F32)
    out[...] = total.astype(BF)


def low_sum(parts):
    return pl.pallas_call(
        low_kernel,
        out_shape=jax.ShapeDtypeStruct(parts.shape[1:], BF),
        in_specs=[pl.BlockSpec(memory_space=pltpu.VMEM)],
        out_specs=pl.BlockSpec(memory_space=pltpu.VMEM),
        compiler_params=params(8),
        cost_estimate=COST,
        name="low_sum",
    )(parts)


def grad_kernel(low_ref, cot_ref, out, low):
    @pl.when(pl.program_id(0) == 0)
    def _():
        low_kernel(low_ref, low)

    for block in range(4):
        out[block] = jnp.dot(
            low[...], cot_ref[:, block * W : (block + 1) * W], preferred_element_type=F32
        )


def grad_partial(low_parts, cotangent):
    tokens, features = cotangent.shape
    ranks = low_parts.shape[1]
    return pl.pallas_call(
        grad_kernel,
        out_shape=pltpu.HBM((features // W, ranks, W), F32),
        grid=(features // (4 * W),),
        in_specs=[
            pl.BlockSpec(low_parts.shape, lambda i: (0, 0, 0)),
            pl.BlockSpec((tokens, 4 * W), lambda i: (0, i)),
        ],
        out_specs=pl.BlockSpec((4, ranks, W), lambda i: (i, 0, 0)),
        scratch_shapes=[pltpu.VMEM((ranks, tokens), BF)],
        compiler_params=params(8),
        cost_estimate=COST,
        name="grad_partial",
    )(low_parts, in_hbm(cotangent))


def moments_kernel(grads, first, second, new_first, new_second, normed):
    grad = grads[0]
    for s in range(1, 16):
        grad = grad + grads[s]
    one = 0.9 * first[...] + 0.1 * grad
    two = 0.999 * second[...] + 0.001 * grad * grad
    new_first[...] = one
    new_second[...] = two
    first_fix = 1.0 - 0.9**STEP
    second_fix = 1.0 - 0.999**STEP
    step = (one / first_fix / (jnp.sqrt(two / second_fix) + 1e-08)).astype(BF)
    for s in range(16):
        normed[s] = step


def moments(grads, first, second):
    full = pl.BlockSpec(memory_space=pltpu.VMEM)
    return pl.pallas_call(
        moments_kernel,
        out_shape=[jax.ShapeDtypeStruct(first.shape, F32)] * 2
        + [jax.ShapeDtypeStruct((16, *first.shape), BF)],
        in_specs=[full] * 3,
        out_specs=[full] * 3,
        compiler_params=params(8),
        cost_estimate=LIGHT,
        name="moments",
    )(grads, first, second)


def act_kernel(order, cot_ref, *refs):
    w_refs, out_ref = refs[:16], refs[16]
    cots, wide, total, cot_sems, w_sems = refs[17:]
    span = 4 * W

    def cot_part(i):
        at = pl.multiple_of(order[i] * span, span)
        return pltpu.make_async_copy(cot_ref.at[:, pl.ds(at, span)], cots.at[i], cot_sems.at[i])

    def shard(i, slot):
        at = pl.multiple_of(order[4 + slot] * W, W)
        return pltpu.make_async_copy(
            w_refs[4 * i + slot], wide.at[i, :, pl.ds(at, W)], w_sems.at[i, slot]
        )

    for i in range(4):
        for slot in range(4):
            shard(i, slot).start()
        cot_part(i).start()
    for i in range(4):
        for slot in range(4):
            shard(i, slot).wait()
        cot_part(i).wait()
        product = lax.dot_general(
            cots[i], wide[i], (((1,), (1,)), ((), ())), preferred_element_type=F32
        )
        if i == 0:
            total[...] = product
        elif i < 3:
            total[...] += product
        else:
            out_ref[...] = (total[...] + product).astype(BF)


def act(cotangent, blocks, order):
    tokens, features = cotangent.shape
    flat = [w for four in blocks for w in four]
    full = flat[0].shape[0]
    anywhere = pl.BlockSpec(memory_space=pl.ANY)
    return pl.pallas_call(
        act_kernel,
        out_shape=jax.ShapeDtypeStruct((tokens, full), BF),
        grid_spec=pltpu.PrefetchScalarGridSpec(
            num_scalar_prefetch=1,
            grid=(1,),
            in_specs=[anywhere] * 17,
            out_specs=pl.BlockSpec((tokens, full), lambda i, s: (0, 0)),
            scratch_shapes=[
                pltpu.VMEM((4, tokens, 4 * W), BF),
                pltpu.VMEM((4, full, 4 * W), BF),
                pltpu.VMEM((tokens, full), F32),
                pltpu.SemaphoreType.DMA((4,)),
                pltpu.SemaphoreType.DMA((4, 4)),
            ],
        ),
        compiler_params=params(30),
        cost_estimate=COST,
        name="act_grad",
    )(order, in_hbm(cotangent), *flat)


def on_device(hidden, cotangent, weight, basis, first_moment, second_moment):
    zh, x, y, zl, c = (lax.axis_index(a) for a in AXES)
    tokens = hidden.shape[0]
    half = tokens // 2

    low_part = lax.dot_general(
        basis, hidden, (((0,), (1,)), ((), ())), preferred_element_type=F32
    ).astype(BF)
    low_part = low_part.reshape(4, 4, 32, tokens).transpose(1, 0, 2, 3)

    side = shift(weight, "zl", 1)
    next0, prev0 = shift(weight, "y", -1), shift(weight, "y", 1)
    low_x = swap(after(low_part, weight), "x")
    side = after(side, low_part, next0, prev0)
    next1, prev1 = shift(side, "y", -1), shift(side, "y", 1)

    def both_cores(own, other):
        return own, shift(own, "c", 1), other, shift(other, "c", 1)

    dest = [2 * (zl ^ (s // 2)) + (c ^ (s % 2)) for s in range(4)]
    goals = [(x + k) % 4 for k in (1, 2, 3, 0)]
    slot_of = jnp.stack([2 * ((g // 2) ^ zl) + ((g % 2) ^ c) for g in goals]).astype(jnp.int32)
    place = jnp.stack([(y + k - zh + 3) % 4 for k in range(4)]).astype(jnp.int32)

    slots = {0: both_cores(weight, side)}
    next0c, prev0c = shift(after(next0, low_part), "c", 1), shift(after(prev0, low_part), "c", 1)
    part0 = partials(after(hidden, next0c, prev0c, low_x), [slots[0]], slot_of, 0, tokens)
    sum0 = spread(part0, "x")
    next1c, prev1c = shift(after(next1, *part0), "c", 1), shift(after(prev1, *part0), "c", 1)
    slots[1] = next0, next0c, next1, next1c
    slots[3] = prev0, prev0c, prev1, prev1c
    far0 = shift(after(next0, next1c, prev1c, *part0), "y", -1)
    far1 = shift(after(prev1, next1c, prev1c, *part0), "y", 1)
    near = [slots[1], slots[3]]
    part1 = partials(after(hidden, *part0), near, slot_of, 0, tokens)
    sum1 = spread(part1, "x")
    slots[2] = both_cores(after(far0, *sum0[1:]), after(far1, *sum0[1:]))
    low_z = swap(low_sum(after(low_x, *part1)), "zh")
    part2 = partials(after(hidden, *part1), [slots[2]], slot_of, 0, half)
    sum2 = spread(part2, "x")
    grad_part = grad_partial(after(low_z, *part2), cotangent)
    grad_all = swap(grad_part, FSDP)
    part3 = partials(after(hidden, grad_part, sum1[1], *part2), [slots[2]], slot_of, half, half)
    sum3 = spread(part3, "x")

    new_first, new_second, normed = moments(grad_all, first_moment, second_moment)
    normed_all = swap(normed, DP)

    order = jnp.stack([(y + off) % 4 for off in slots] + dest).astype(jnp.int32)
    zparts = regroup([(sum0, (0,)), (sum1, (1, 3)), (sum2, (2,)), (sum3, (2,))], after(place, normed))
    act_grad = act(after(cotangent, *zparts), [[in_hbm(w) for w in four] for four in slots.values()], order)
    normed_all = after(normed_all, *zparts).reshape(-1, W)
    update = jnp.dot(basis, normed_all, preferred_element_type=F32).astype(BF)
    output = finish(spread(zparts, "zh"))
    return output, act_grad, new_first, new_second, update


def solution(mesh):
    fine = Mesh(mesh.devices.reshape(tuple(SIZE[a] for a in AXES)), AXES)
    in_specs = (
        P(FSDP, DP),
        P(FSDP, None),
        P(DP, FSDP),
        P(DP, None),
        P(DP, FSDP),
        P(DP, FSDP),
    )
    out_specs = (P(FSDP, DP), P(FSDP, DP), P(DP, FSDP), P(DP, FSDP), P(DP, FSDP))
    return jax.shard_map(
        on_device, mesh=fine, in_specs=in_specs, out_specs=out_specs, check_vma=False
    )
```

```python
import functools

import jax
import jax.numpy as jnp
from jax import lax
from jax.experimental import pallas as pl
from jax.experimental.pallas import tpu as pltpu
from jax.sharding import Mesh
from jax.sharding import PartitionSpec as P

STEP = 20
BF = jnp.bfloat16
F32 = jnp.float32
AXES = ("zh", "x", "y", "zl", "c")
SIZE = dict(zh=4, x=4, y=4, zl=2, c=2)
FSDP = ("y", "zl", "c")
DP = ("zh", "x")
W = 256
MIB = 1024 * 1024
LIGHT = pl.CostEstimate(flops=1 << 20, bytes_accessed=1 << 16, transcendentals=0)
COST = pl.CostEstimate(flops=1 << 33, bytes_accessed=1 << 25, transcendentals=0)


def shift(array, axis, by):
    n = SIZE[axis]
    return lax.ppermute(array, axis, [(i, (i + by) % n) for i in range(n)])


def swap(array, axes):
    return lax.all_to_all(array, axes, 0, 0, tiled=True)


def after(value, *others):
    return lax.optimization_barrier((value, *others))[0]


def in_hbm(value):
    return pltpu.with_memory_space_constraint(value, pltpu.HBM)


def params(limit):
    return pltpu.CompilerParams(vmem_limit_bytes=limit * MIB)


def partial_kernel(m, start, slot_of, h_ref, *refs):
    w_refs, outs = refs[: 4 * m], refs[4 * m : 4 * m + 4]
    mine, wide, held, h_sem, w_sems, out_sems = refs[4 * m + 4 :]

    def load(k, block, slot):
        return pltpu.make_async_copy(
            w_refs[4 * block + slot], wide.at[k, :, pl.ds(block * W, W)], w_sems.at[k, block]
        )

    def store(k):
        return pltpu.make_async_copy(held.at[k], outs[k], out_sems.at[k])

    hidden = pltpu.make_async_copy(h_ref.at[pl.ds(start, mine.shape[0])], mine, h_sem)
    hidden.start()
    for k in range(4):
        for block in range(m):
            for slot in range(4):

                @pl.when(slot_of[k] == slot)
                def _(k=k, block=block, slot=slot):
                    load(k, block, slot).start()

    hidden.wait()
    for k in range(4):
        for block in range(m):
            load(k, block, 0).wait()
        held[k] = jnp.dot(mine[...], wide[k], preferred_element_type=F32).astype(BF)
        store(k).start()
    for k in range(4):
        store(k).wait()


def partials(hidden, blocks, slot_of, start, rows):
    full = hidden.shape[1]
    m = len(blocks)
    flat = [w for four in blocks for w in four]
    anywhere = pl.BlockSpec(memory_space=pl.ANY)
    return pl.pallas_call(
        functools.partial(partial_kernel, m, start),
        out_shape=[pltpu.HBM((rows, m * W), BF)] * 4,
        grid_spec=pltpu.PrefetchScalarGridSpec(
            num_scalar_prefetch=1,
            grid=(1,),
            in_specs=[anywhere] * (1 + 4 * m),
            out_specs=[anywhere] * 4,
            scratch_shapes=[
                pltpu.VMEM((rows, full), BF),
                pltpu.VMEM((4, full, m * W), BF),
                pltpu.VMEM((4, rows, m * W), BF),
                pltpu.SemaphoreType.DMA,
                pltpu.SemaphoreType.DMA((4, m)),
                pltpu.SemaphoreType.DMA((4,)),
            ],
        ),
        compiler_params=params(20),
        cost_estimate=COST,
        name="partials",
    )(slot_of, in_hbm(hidden), *flat)


def regroup_kernel(offsets, place, *refs):
    outs = refs[4 * len(offsets) :]
    i = pl.program_id(0)

    def add(group, offs):
        four = refs[4 * group : 4 * group + 4]
        total = four[0][...].astype(F32)
        for ref in four[1:]:
            total += ref[...].astype(F32)
        total = total.astype(BF)
        for block, off in enumerate(offs):
            for which in range(4):

                @pl.when(place[off] == which)
                def _(total=total, block=block, which=which):
                    outs[which][...] = total[:, block * W : (block + 1) * W]

    for group, offs in enumerate(offsets[:-2]):
        add(group, offs)
    pl.when(i < 2)(lambda: add(len(offsets) - 2, offsets[-2]))
    pl.when(i >= 2)(lambda: add(len(offsets) - 1, offsets[-1]))


def regroup(groups, place):
    rows = groups[0][0][0].shape[0]
    tile = rows // 4
    specs, arrays = [], []
    row_of = [lambda i: i] * (len(groups) - 2) + [lambda i: jnp.minimum(i, 1), lambda i: jnp.maximum(i - 2, 0)]
    for (four, offs), row in zip(groups, row_of):
        specs += [pl.BlockSpec((tile, len(offs) * W), lambda i, s, row=row: (row(i), 0))] * 4
        arrays += four
    return pl.pallas_call(
        functools.partial(regroup_kernel, [offs for _, offs in groups]),
        out_shape=[pltpu.HBM((rows, W), BF)] * 4,
        grid_spec=pltpu.PrefetchScalarGridSpec(
            num_scalar_prefetch=1,
            grid=(rows // tile,),
            in_specs=specs,
            out_specs=[pl.BlockSpec((tile, W), lambda i, s: (i, 0))] * 4,
        ),
        compiler_params=params(16),
        cost_estimate=COST,
        name="regroup",
    )(place, *arrays)


def spread(parts, axis):
    got = [parts[3]] + [shift(parts[k - 1], axis, k) for k in (1, 3, 2)]
    return [in_hbm(part) for part in got] if axis == "x" else got


def finish_kernel(a, b, c, d, out):
    total = a[...].astype(F32) + b[...].astype(F32) + c[...].astype(F32) + d[...].astype(F32)
    out[...] = total.astype(BF)


def finish(parts):
    rows = parts[0].shape[0]
    tile = rows // 2
    spec = pl.BlockSpec((tile, W), lambda i: (i, 0))
    return pl.pallas_call(
        finish_kernel,
        out_shape=jax.ShapeDtypeStruct((rows, W), BF),
        grid=(2,),
        in_specs=[spec] * 4,
        out_specs=spec,
        compiler_params=params(12),
        cost_estimate=LIGHT,
        name="finish",
    )(*parts)


def low_kernel(parts, out):
    total = parts[0].astype(F32)
    for s in range(1, 4):
        total += parts[s].astype(F32)
    out[...] = total.astype(BF)


def low_sum(parts):
    return pl.pallas_call(
        low_kernel,
        out_shape=jax.ShapeDtypeStruct(parts.shape[1:], BF),
        in_specs=[pl.BlockSpec(memory_space=pltpu.VMEM)],
        out_specs=pl.BlockSpec(memory_space=pltpu.VMEM),
        compiler_params=params(8),
        cost_estimate=COST,
        name="low_sum",
    )(parts)


def grad_kernel(low_ref, cot_ref, out, low):
    @pl.when(pl.program_id(0) == 0)
    def _():
        low_kernel(low_ref, low)

    for block in range(4):
        out[block] = jnp.dot(
            low[...], cot_ref[:, block * W : (block + 1) * W], preferred_element_type=F32
        )


def grad_partial(low_parts, cotangent):
    tokens, features = cotangent.shape
    ranks = low_parts.shape[1]
    return pl.pallas_call(
        grad_kernel,
        out_shape=pltpu.HBM((features // W, ranks, W), F32),
        grid=(features // (4 * W),),
        in_specs=[
            pl.BlockSpec(low_parts.shape, lambda i: (0, 0, 0)),
            pl.BlockSpec((tokens, 4 * W), lambda i: (0, i)),
        ],
        out_specs=pl.BlockSpec((4, ranks, W), lambda i: (i, 0, 0)),
        scratch_shapes=[pltpu.VMEM((ranks, tokens), BF)],
        compiler_params=params(8),
        cost_estimate=COST,
        name="grad_partial",
    )(low_parts, in_hbm(cotangent))


def moments_kernel(grads, first, second, new_first, new_second, normed):
    grad = grads[0]
    for s in range(1, 16):
        grad = grad + grads[s]
    one = 0.9 * first[...] + 0.1 * grad
    two = 0.999 * second[...] + 0.001 * grad * grad
    new_first[...] = one
    new_second[...] = two
    first_fix = 1.0 - 0.9**STEP
    second_fix = 1.0 - 0.999**STEP
    step = (one / first_fix / (jnp.sqrt(two / second_fix) + 1e-08)).astype(BF)
    for s in range(16):
        normed[s] = step


def moments(grads, first, second):
    full = pl.BlockSpec(memory_space=pltpu.VMEM)
    return pl.pallas_call(
        moments_kernel,
        out_shape=[jax.ShapeDtypeStruct(first.shape, F32)] * 2
        + [jax.ShapeDtypeStruct((16, *first.shape), BF)],
        in_specs=[full] * 3,
        out_specs=[full] * 3,
        compiler_params=params(8),
        cost_estimate=LIGHT,
        name="moments",
    )(grads, first, second)


def act_kernel(order, cot_ref, *refs):
    w_refs, out_ref = refs[:16], refs[16]
    cots, wide, total, cot_sems, w_sems = refs[17:]
    span = 4 * W

    def cot_part(i):
        at = pl.multiple_of(order[i] * span, span)
        return pltpu.make_async_copy(cot_ref.at[:, pl.ds(at, span)], cots.at[i], cot_sems.at[i])

    def shard(i, slot):
        at = pl.multiple_of(order[4 + slot] * W, W)
        return pltpu.make_async_copy(
            w_refs[4 * i + slot], wide.at[i, :, pl.ds(at, W)], w_sems.at[i, slot]
        )

    for i in range(4):
        for slot in range(4):
            shard(i, slot).start()
        cot_part(i).start()
    for i in range(4):
        for slot in range(4):
            shard(i, slot).wait()
        cot_part(i).wait()
        product = lax.dot_general(
            cots[i], wide[i], (((1,), (1,)), ((), ())), preferred_element_type=F32
        )
        if i == 0:
            total[...] = product
        elif i < 3:
            total[...] += product
        else:
            out_ref[...] = (total[...] + product).astype(BF)


def act(cotangent, blocks, order):
    tokens, features = cotangent.shape
    flat = [w for four in blocks for w in four]
    full = flat[0].shape[0]
    anywhere = pl.BlockSpec(memory_space=pl.ANY)
    return pl.pallas_call(
        act_kernel,
        out_shape=jax.ShapeDtypeStruct((tokens, full), BF),
        grid_spec=pltpu.PrefetchScalarGridSpec(
            num_scalar_prefetch=1,
            grid=(1,),
            in_specs=[anywhere] * 17,
            out_specs=pl.BlockSpec((tokens, full), lambda i, s: (0, 0)),
            scratch_shapes=[
                pltpu.VMEM((4, tokens, 4 * W), BF),
                pltpu.VMEM((4, full, 4 * W), BF),
                pltpu.VMEM((tokens, full), F32),
                pltpu.SemaphoreType.DMA((4,)),
                pltpu.SemaphoreType.DMA((4, 4)),
            ],
        ),
        compiler_params=params(30),
        cost_estimate=COST,
        name="act_grad",
    )(order, in_hbm(cotangent), *flat)


def on_device(hidden, cotangent, weight, basis, first_moment, second_moment):
    zh, x, y, zl, c = (lax.axis_index(a) for a in AXES)
    tokens = hidden.shape[0]
    half = tokens // 2

    low_part = lax.dot_general(
        basis, hidden, (((0,), (1,)), ((), ())), preferred_element_type=F32
    ).astype(BF)
    low_part = low_part.reshape(4, 4, 32, tokens).transpose(1, 0, 2, 3)

    side = shift(weight, "zl", 1)
    next0, prev0 = shift(weight, "y", -1), shift(weight, "y", 1)
    low_x = swap(after(low_part, weight), "x")
    side = after(side, low_part, next0, prev0)
    next1, prev1 = shift(side, "y", -1), shift(side, "y", 1)

    def both_cores(own, other):
        return own, shift(own, "c", 1), other, shift(other, "c", 1)

    dest = [2 * (zl ^ (s // 2)) + (c ^ (s % 2)) for s in range(4)]
    goals = [(x + k) % 4 for k in (1, 2, 3, 0)]
    slot_of = jnp.stack([2 * ((g // 2) ^ zl) + ((g % 2) ^ c) for g in goals]).astype(jnp.int32)
    place = jnp.stack([(y + k - zh + 3) % 4 for k in range(4)]).astype(jnp.int32)

    slots = {0: both_cores(weight, side)}
    next0c, prev0c = shift(after(next0, low_part), "c", 1), shift(after(prev0, low_part), "c", 1)
    part0 = partials(after(hidden, next0c, prev0c, low_x), [slots[0]], slot_of, 0, tokens)
    sum0 = spread(part0, "x")
    next1c, prev1c = shift(after(next1, *part0), "c", 1), shift(after(prev1, *part0), "c", 1)
    slots[1] = next0, next0c, next1, next1c
    slots[3] = prev0, prev0c, prev1, prev1c
    far0 = shift(after(next0, next1c, prev1c, *part0), "y", -1)
    far1 = shift(after(prev1, next1c, prev1c, *part0), "y", 1)
    near = [slots[1], slots[3]]
    part1 = partials(after(hidden, *part0), near, slot_of, 0, tokens)
    sum1 = spread(part1, "x")
    slots[2] = both_cores(after(far0, *sum0[1:]), after(far1, *sum0[1:]))
    low_z = swap(low_sum(after(low_x, *part1)), "zh")
    part2 = partials(after(hidden, *part1), [slots[2]], slot_of, 0, half)
    sum2 = spread(part2, "x")
    grad_part = grad_partial(after(low_z, *part2), cotangent)
    grad_all = swap(grad_part, FSDP)
    part3 = partials(after(hidden, grad_part, *part2), [slots[2]], slot_of, half, half)
    sum3 = spread(part3, "x")

    new_first, new_second, normed = moments(grad_all, first_moment, second_moment)
    normed_all = swap(normed, DP)

    order = jnp.stack([(y + off) % 4 for off in slots] + dest).astype(jnp.int32)
    zparts = regroup([(sum0, (0,)), (sum1, (1, 3)), (sum2, (2,)), (sum3, (2,))], after(place, normed))
    act_grad = act(after(cotangent, *zparts), [[in_hbm(w) for w in four] for four in slots.values()], order)
    normed_all = after(normed_all, *zparts).reshape(-1, W)
    update = jnp.dot(basis, normed_all, preferred_element_type=F32).astype(BF)
    output = finish(spread(zparts, "zh"))
    return output, act_grad, new_first, new_second, update


def solution(mesh):
    fine = Mesh(mesh.devices.reshape(tuple(SIZE[a] for a in AXES)), AXES)
    in_specs = (
        P(FSDP, DP),
        P(FSDP, None),
        P(DP, FSDP),
        P(DP, None),
        P(DP, FSDP),
        P(DP, FSDP),
    )
    out_specs = (P(FSDP, DP), P(FSDP, DP), P(DP, FSDP), P(DP, FSDP), P(DP, FSDP))
    return jax.shard_map(
        on_device, mesh=fine, in_specs=in_specs, out_specs=out_specs, check_vma=False
    )
```
